256 devices in a mesh: dp: 2 (over core), ctx: 8 (over z), resp: 16 (over x, y).
Axes of the slice: x: 4, y: 4, z: 8, core: 2. Of those that a mesh axis runs over, the one named last changes fastest.
Arguments:
- prompt_x: bfloat16 [2, 32768, 4096], P('dp', ('ctx', 'resp')), may hold values from -6 to 6
- prompt_b: bfloat16 [2, 32768, 128], P('dp', ('ctx', 'resp')), may hold values from -0.75 to 0.75
- prompt_dt: float32 [2, 32768, 64], P('dp', ('ctx', 'resp')), may hold values from -6 to 7
- prompt_states: bfloat16 [2, 128, 64, 64, 128], P('dp', ('ctx', 'resp')), may hold values from -6 to 6
- resp_x: bfloat16 [2, 16, 2048, 4096], P('dp', 'resp', 'ctx'), may hold values from -6 to 6
- resp_b: bfloat16 [2, 16, 2048, 128], P('dp', 'resp', 'ctx'), may hold values from -0.75 to 0.75
- resp_c: bfloat16 [2, 16, 2048, 128], P('dp', 'resp', 'ctx'), may hold values from -0.75 to 0.75
- resp_dt: float32 [2, 16, 2048, 64], P('dp', 'resp', 'ctx'), may hold values from -6 to 7
- grad_out: bfloat16 [2, 16, 2048, 4096], P('dp', 'resp', 'ctx'), may hold values from -0.625 to 0.625
- lengths: int32 [2, 16], P('dp', 'resp'), may hold values from 256 to 2048, as said below
- advantages: float32 [2, 16], P('dp', 'resp'), may hold values from -6 to 6
- dt_bias: float32 [64], replicated, may hold values from -1 to 0.5
- a_log: float32 [64], replicated, may hold values from -20 to -2
- skip: float32 [64], replicated, may hold values from 0.5 to 1.5
Outputs:
- prompt_dx: bfloat16 [2, 32768, 4096], P('dp', ('ctx', 'resp'))
- prompt_db: float32 [2, 32768, 128], P('dp', ('ctx', 'resp'))
- prompt_ddt: float32 [2, 32768, 64], P('dp', ('ctx', 'resp'))
- resp_dx: bfloat16 [2, 16, 2048, 4096], P('dp', 'resp', 'ctx')
- resp_db: float32 [2, 16, 2048, 128], P('dp', 'resp', 'ctx')
- resp_dc: float32 [2, 16, 2048, 128], P('dp', 'resp', 'ctx')
- resp_ddt: float32 [2, 16, 2048, 64], P('dp', 'resp', 'ctx')
- grad_bias: float32 [64], replicated
- grad_alog: float32 [64], replicated
- grad_skip: float32 [64], replicated
The draws below stay inside these ranges and needn't reach their ends.
Inputs may be any that keep to these rules, and one draw needn't show every extreme that they name: `lengths`: at least 256; in every group one response has exactly 2048 tokens.
All inputs are finite; a program needn't handle non-finite values.
Results may differ from the reference program's by a relative error of at most 0.0011.
Values sent between devices are 32-bit elements; how exact they have to be, the bound alone decides.
A program may use at most 192 MiB of HBM per device.

```python
import math
import jax
import jax.numpy as jnp
from jax import lax

HEADS = 64
HEAD_DIM = 64
STATE = 128
STRETCH = 256
GROUPS = 2
RESPS = 16
PBLOCKS = 128
PLEN = 32768
RLEN = 2048
WIDTH = 4096


def draw_lengths(key, part):
    key = jax.random.fold_in(key, 11)
    first_key, second_key = jax.random.split(key)
    drawn = jax.random.randint(first_key, (GROUPS, RESPS), RLEN // 8, RLEN + 1)
    longest = jax.random.randint(second_key, (GROUPS,), 0, RESPS)
    chosen = jnp.arange(RESPS)[None, :] == longest[:, None]
    return jnp.where(chosen, RLEN, drawn).astype(jnp.int32)


def draw_a_log(key, part):
    key = jax.random.fold_in(key, 23)
    span_total = PLEN + RLEN
    lower = math.log(0.01 / span_total)
    upper = math.log(0.05)
    fraction = jax.random.uniform(key, (HEADS,), jnp.float32)
    return (lower + fraction * (upper - lower)).astype(jnp.float32)


def stretch_steps(key, shape, low, high, noise):
    lead = tuple(shape[:-2])
    count = shape[-2] // STRETCH
    offset_key, noise_key = jax.random.split(key)
    offset = jax.random.uniform(offset_key, lead + (count, 1, shape[-1]), jnp.float32, low, high)
    jitter = noise * jax.random.normal(noise_key, lead + (count, STRETCH, shape[-1]), jnp.float32)
    jitter = jnp.clip(jitter, -3.0 * noise, 3.0 * noise)
    return (offset + jitter).reshape(shape).astype(jnp.float32)


def draw_prompt_dt(key, part):
    key = jax.random.fold_in(key, 37)
    return stretch_steps(key, (GROUPS, PLEN, HEADS), -2.0, 2.5, 0.5)


def draw_resp_dt(key, part):
    key = jax.random.fold_in(key, 41)
    return stretch_steps(key, (GROUPS, RESPS, RLEN, HEADS), -2.0, 2.5, 0.5)


def levels(own_key, shape, cuts, least, top_value):
    factor_of = 1.0
    for axis_at, blocks in cuts:
        draws = jax.random.uniform(jax.random.fold_in(jax.random.fold_in(own_key, 6), axis_at), (blocks,), jnp.float32, least / len(cuts), top_value / len(cuts))
        factor_of = factor_of * jnp.repeat(jnp.exp(draws), shape[axis_at] // blocks).reshape((-1,) + (1,) * (len(shape) - 1 - axis_at))
    return factor_of


def normal_values(own_key, shape, deviation, limit, shards=(), kind=jnp.bfloat16):
    values = jax.random.normal(own_key, shape, jnp.float32) * deviation
    if len(shards) > 0:
        values = levels(own_key, shape, shards, -0.22, 0.18) * values
    return jnp.clip(values, min=-limit, max=limit).astype(kind)


def setup_inputs(seed: int = 0) -> dict:
    streams_of = jax.random.split(jax.random.key(seed), 15)
    prompt_x = normal_values(streams_of[0], (GROUPS, PLEN, WIDTH), 1.0, 6.0, ((0, 2), (1, 128)))
    prompt_b = normal_values(streams_of[1], (GROUPS, PLEN, STATE), 0.125, 0.75, ((0, 2), (1, 128)))
    prompt_dt = draw_prompt_dt(jax.random.fold_in(streams_of[14], 71), 0)
    prompt_states = normal_values(streams_of[3], (GROUPS, PBLOCKS, HEADS, HEAD_DIM, STATE), 1.0, 6.0, ((0, 2), (1, 128)))
    resp_x = normal_values(streams_of[4], (GROUPS, RESPS, RLEN, WIDTH), 1.0, 6.0, ((0, 2), (1, 16), (2, 8)))
    resp_b = normal_values(streams_of[5], (GROUPS, RESPS, RLEN, STATE), 0.125, 0.75, ((0, 2), (1, 16), (2, 8)))
    resp_c = normal_values(streams_of[6], (GROUPS, RESPS, RLEN, STATE), 0.125, 0.75, ((0, 2), (1, 16), (2, 8)))
    resp_dt = draw_resp_dt(jax.random.fold_in(streams_of[14], 71), 0)
    grad_out = normal_values(streams_of[8], (GROUPS, RESPS, RLEN, WIDTH), 0.1, 0.625, ((0, 2), (1, 16), (2, 8)))
    lengths = draw_lengths(jax.random.fold_in(streams_of[14], 71), 0)
    advantages = normal_values(streams_of[10], (GROUPS, RESPS), 1.0, 6.0, ((0, 2), (1, 16)), jnp.float32)
    dt_bias = jnp.clip(jax.random.uniform(streams_of[11], (HEADS,), jnp.float32, -1.0, 0.5), -1.0, 0.5)
    a_log = draw_a_log(jax.random.fold_in(streams_of[14], 71), 0)
    skip = jnp.clip(jax.random.uniform(streams_of[13], (HEADS,), jnp.float32, 0.5, 1.5), 0.5, 1.5)
    return dict(prompt_x=prompt_x, prompt_b=prompt_b, prompt_dt=prompt_dt, prompt_states=prompt_states, resp_x=resp_x, resp_b=resp_b, resp_c=resp_c, resp_dt=resp_dt, grad_out=grad_out, lengths=lengths, advantages=advantages, dt_bias=dt_bias, a_log=a_log, skip=skip)


precise = lax.Precision.HIGHEST

def decay_terms(raw_step, step_bias, log_rate):
    step_size = jax.nn.softplus(raw_step + step_bias)
    running = jnp.cumsum(-jnp.exp(log_rate) * step_size, axis=0)
    return (step_size, running)

def block_output(inputs, b_proj, c_proj, raw_step, step_bias, log_rate, skip_gain, state_in):
    step_size, running = decay_terms(raw_step, step_bias, log_rate)
    tokens_in = inputs.shape[0]
    causal = jnp.arange(tokens_in)[:, None] >= jnp.arange(tokens_in)[None, :]
    spread = running.T[:, :, None] - running.T[:, None, :]
    kernel = jnp.exp(jnp.where(causal[None], spread, -jnp.inf))
    scores = jnp.dot(c_proj, b_proj.T, precision=precise)
    weights = kernel * scores[None] * step_size.T[:, None, :]
    within = jnp.einsum('hts,shp->thp', weights, inputs, precision=precise)
    carried = jnp.exp(running)[:, :, None] * jnp.einsum('tn,hpn->thp', c_proj, state_in, precision=precise)
    return within + carried + skip_gain[None, :, None] * inputs

def block_state(inputs, b_proj, raw_step, step_bias, log_rate, state_in):
    step_size, running = decay_terms(raw_step, step_bias, log_rate)
    closing = running[-1]
    toward = jnp.exp(closing[None, :] - running) * step_size
    driven = toward[:, :, None] * inputs
    return jnp.exp(closing)[:, None, None] * state_in + jnp.einsum('shp,sn->hpn', driven, b_proj, precision=precise)

def response_block(inputs, b_proj, c_proj, raw_step, step_bias, log_rate, skip_gain, state_in, cotangent, state_grad):

    def forward(inputs, b_proj, c_proj, raw_step, step_bias, log_rate, skip_gain, state_in):
        return (block_output(inputs, b_proj, c_proj, raw_step, step_bias, log_rate, skip_gain, state_in), block_state(inputs, b_proj, raw_step, step_bias, log_rate, state_in))
    unused, pullback = jax.vjp(forward, inputs, b_proj, c_proj, raw_step, step_bias, log_rate, skip_gain, state_in)
    return pullback((cotangent, state_grad))

def prompt_block(inputs, b_proj, raw_step, step_bias, log_rate, state_in, state_grad):

    def forward(inputs, b_proj, raw_step, step_bias, log_rate):
        return block_state(inputs, b_proj, raw_step, step_bias, log_rate, state_in)
    unused, pullback = jax.vjp(forward, inputs, b_proj, raw_step, step_bias, log_rate)
    return pullback(state_grad)

def by_heads(values, blocks):
    old_shape = values.shape
    reshaped = values.reshape((old_shape[0], blocks, old_shape[1] // blocks) + old_shape[2:])
    return jnp.moveaxis(reshaped, 1, 0)

def from_heads(values):
    shifted = jnp.moveaxis(values, 0, 1)
    return shifted.reshape((shifted.shape[0], shifted.shape[1] * shifted.shape[2]) + shifted.shape[3:])

def head_first(values, blocks):
    return values.reshape((blocks, values.shape[0] // blocks) + values.shape[1:])

def head_back(values):
    return values.reshape((values.shape[0] * values.shape[1],) + values.shape[2:])

def response_grads(inputs, b_proj, c_proj, raw_step, step_bias, log_rate, skip_gain, state_in, cotangent, state_grad):
    head_count = inputs.shape[1]
    blocks = head_count // math.gcd(head_count, 16)

    def per_block(pieces):
        return response_block(pieces[0], b_proj, c_proj, pieces[1], pieces[2], pieces[3], pieces[4], pieces[5], pieces[6], pieces[7])
    results = lax.map(per_block, (by_heads(inputs, blocks), by_heads(raw_step, blocks), head_first(step_bias, blocks), head_first(log_rate, blocks), head_first(skip_gain, blocks), head_first(state_in, blocks), by_heads(cotangent, blocks), head_first(state_grad, blocks)))
    return (from_heads(results[0]), lax.optimization_barrier(jnp.sum(results[1], axis=0)), lax.optimization_barrier(jnp.sum(results[2], axis=0)), from_heads(results[3]), head_back(results[4]), head_back(results[5]), head_back(results[6]), head_back(results[7]))

def prompt_grads(inputs, b_proj, raw_step, step_bias, log_rate, state_in, state_grad):
    head_count = inputs.shape[1]
    blocks = head_count // math.gcd(head_count, 16)

    def per_block(pieces):
        return prompt_block(pieces[0], b_proj, pieces[1], pieces[2], pieces[3], pieces[4], pieces[5])
    results = lax.map(per_block, (by_heads(inputs, blocks), by_heads(raw_step, blocks), head_first(step_bias, blocks), head_first(log_rate, blocks), head_first(state_in, blocks), head_first(state_grad, blocks)))
    return (from_heads(results[0]), lax.optimization_barrier(jnp.sum(results[1], axis=0)), from_heads(results[2]), head_back(results[3]), head_back(results[4]))

def reference(prompt_x, prompt_b, prompt_dt, prompt_states, resp_x, resp_b, resp_c, resp_dt, grad_out, lengths, advantages, dt_bias, a_log, skip):
    answer_blocks = RLEN // STRETCH
    outs_pdx, outs_pdb, outs_pdt = ([], [], [])
    outs_rdx, outs_rdb, outs_rdc, outs_rdt = ([], [], [], [])
    sum_bias = jnp.zeros((HEADS,), jnp.float32)
    sum_alog = jnp.zeros((HEADS,), jnp.float32)
    sum_skip = jnp.zeros((HEADS,), jnp.float32)
    for group_idx in range(GROUPS):
        block_x = prompt_x[group_idx].astype(jnp.float32).reshape(PBLOCKS, STRETCH, HEADS, HEAD_DIM)
        block_b = prompt_b[group_idx].astype(jnp.float32).reshape(PBLOCKS, STRETCH, STATE)
        block_dt = prompt_dt[group_idx].reshape(PBLOCKS, STRETCH, HEADS)
        saved = prompt_states[group_idx].astype(jnp.float32)
        end_state = block_state(block_x[PBLOCKS - 1], block_b[PBLOCKS - 1], block_dt[PBLOCKS - 1], dt_bias, a_log, saved[PBLOCKS - 1])

        def respond(pieces):
            ans_x = pieces[0].astype(jnp.float32).reshape(answer_blocks, STRETCH, HEADS, HEAD_DIM)
            ans_b = pieces[1].astype(jnp.float32).reshape(answer_blocks, STRETCH, STATE)
            ans_c = pieces[2].astype(jnp.float32).reshape(answer_blocks, STRETCH, STATE)
            ans_dt = pieces[3].reshape(answer_blocks, STRETCH, HEADS)
            factor = pieces[6] * RLEN / pieces[5].astype(jnp.float32)
            in_range = jnp.arange(RLEN) < pieces[5]
            cotangent = pieces[4].astype(jnp.float32) * jnp.where(in_range, factor, 0.0)[:, None]
            cotangent = cotangent.reshape(answer_blocks, STRETCH, HEADS, HEAD_DIM)

            def advance(state_now, parts):
                return (block_state(parts[0], parts[1], parts[2], dt_bias, a_log, state_now), state_now)
            unused, starts = lax.scan(advance, end_state, (ans_x, ans_b, ans_dt))

            def retreat(state_grad, parts):
                results = response_grads(parts[0], parts[1], parts[2], parts[3], dt_bias, a_log, skip, parts[4], parts[5], state_grad)
                return (results[7], results[:7])
            start_grad, grads = lax.scan(retreat, jnp.zeros((HEADS, HEAD_DIM, STATE), jnp.float32), (ans_x, ans_b, ans_c, ans_dt, starts, cotangent), reverse=True)
            return (start_grad, grads)
        start_grads, grads = lax.map(respond, (resp_x[group_idx], resp_b[group_idx], resp_c[group_idx], resp_dt[group_idx], grad_out[group_idx], lengths[group_idx], advantages[group_idx]))
        seed_grad = lax.optimization_barrier(jnp.sum(start_grads, axis=0))

        def block_decay(raw_step):
            return jnp.exp(decay_terms(raw_step, dt_bias, a_log)[1][-1])
        decays = jax.vmap(block_decay)(block_dt)
        inclusive = jnp.cumprod(decays[::-1], axis=0)[::-1]
        follow = jnp.concatenate([inclusive[1:], jnp.ones((1, HEADS), jnp.float32)], axis=0)

        def backfill(parts):
            return prompt_grads(parts[0], parts[1], parts[2], dt_bias, a_log, parts[3], parts[4][:, None, None] * seed_grad)
        prompt_results = lax.map(backfill, (block_x, block_b, block_dt, saved, follow))
        outs_pdx.append(prompt_results[0].reshape(PLEN, WIDTH).astype(jnp.bfloat16))
        outs_pdb.append(prompt_results[1].reshape(PLEN, STATE))
        outs_pdt.append(prompt_results[2].reshape(PLEN, HEADS))
        outs_rdx.append(grads[0].reshape(RESPS, RLEN, WIDTH).astype(jnp.bfloat16))
        outs_rdb.append(grads[1].reshape(RESPS, RLEN, STATE))
        outs_rdc.append(grads[2].reshape(RESPS, RLEN, STATE))
        outs_rdt.append(grads[3].reshape(RESPS, RLEN, HEADS))
        sum_bias = sum_bias + lax.optimization_barrier(jnp.sum(prompt_results[3], axis=0)) + lax.optimization_barrier(jnp.sum(grads[4], axis=(0, 1)))
        sum_alog = sum_alog + lax.optimization_barrier(jnp.sum(prompt_results[4], axis=0)) + lax.optimization_barrier(jnp.sum(grads[5], axis=(0, 1)))
        sum_skip = sum_skip + lax.optimization_barrier(jnp.sum(grads[6], axis=(0, 1)))
    return (jnp.stack(outs_pdx), jnp.stack(outs_pdb), jnp.stack(outs_pdt), jnp.stack(outs_rdx), jnp.stack(outs_rdb), jnp.stack(outs_rdc), jnp.stack(outs_rdt), sum_bias, sum_alog, sum_skip)
```

```python
import functools

import jax
import jax.numpy as jnp
from jax import lax
from jax.experimental import pallas as pl
from jax.experimental.pallas import tpu as pltpu
from jax.sharding import PartitionSpec as P

MESH = pl.DeviceIdType.MESH
F32 = jnp.float32
BF16 = jnp.bfloat16
TOK = 256
LANES = 256
PER = 4
NH = 64
HD = 64
NS = 128
CHUNKS = 16
PAIRS = 32
LIMIT = 56 * 1024 * 1024


def nn(a, b):
    return lax.dot_general(a, b, (((1,), (0,)), ((), ())), preferred_element_type=F32)


def nt(a, b):
    return lax.dot_general(a, b, (((1,), (1,)), ((), ())), preferred_element_type=F32)


def split2(v):
    hi = v.astype(BF16)
    return hi, (v - hi.astype(F32)).astype(BF16)


def split3(v):
    hi = v.astype(BF16)
    rest = v - hi.astype(F32)
    mid = rest.astype(BF16)
    return hi, mid, (rest - mid.astype(F32)).astype(BF16)


def exact_nn(tri, v):
    hi, mid, lo = split3(v)
    return nn(tri, hi) + (nn(tri, mid) + nn(tri, lo))


def iota(shape, dim):
    return lax.broadcasted_iota(jnp.int32, shape, dim)


def lower():
    return jnp.where(iota((TOK, TOK), 0) >= iota((TOK, TOK), 1), 1.0, 0.0).astype(BF16)


def upper():
    return jnp.where(iota((TOK, TOK), 0) <= iota((TOK, TOK), 1), 1.0, 0.0).astype(BF16)


def spreader(c, rows):
    head = iota((rows, LANES), 0) & (NH - 1)
    lane = iota((rows, LANES), 1) >> 6
    return jnp.where(head == lane + c * PER, 1.0, 0.0).astype(BF16)


def steps(dt, bias, alog):
    z = dt + bias
    d = jnp.maximum(z, 0.0) + jnp.log1p(jnp.exp(-jnp.abs(z)))
    rate = -jnp.exp(alog)
    a = exact_nn(lower(), rate * d)
    return z, d, rate, a


def cat2(v):
    hi, lo = split2(v)
    return jnp.concatenate([hi, lo], axis=1)


def by_head(v, spread):
    hi, lo = split2(v)
    return nt(hi, spread) + nt(lo, spread)


def fold8(v):
    total = v[0:8]
    for at in range(8, v.shape[0], 8):
        total = total + v[at : at + 8]
    return total


def row_mask(length_ref):
    position = lax.axis_index("ctx") * TOK + iota((TOK, 1), 0)
    return jnp.where(position < length_ref[0, 0], 1.0, 0.0)


def first_kernel(
    len_ref, rx_ref, rb_ref, rc_ref, rdt_ref, gy_ref, px_ref, pb_ref, pdt_ref, ps_ref, bias_ref, alog_ref,
    fresh_ref, entry_ref, end_ref,
    wcat, ecat, bt, ct, pwcat, pecat, pbt,
):
    c = pl.program_id(0)
    last = (lax.axis_index("ctx") == lax.axis_size("ctx") - 1) & (
        lax.axis_index("resp") == lax.axis_size("resp") - 1
    )

    @pl.when(c == 0)
    def _():
        bias, alog = bias_ref[...], alog_ref[...]
        _, d, _, a = steps(rdt_ref[...], bias, alog)
        wcat[...] = cat2(jnp.exp(a[TOK - 1 :, :] - a) * d)
        ecat[...] = cat2(jnp.exp(a) * row_mask(len_ref))
        bt[...] = rb_ref[...].astype(F32).T.astype(BF16)
        ct[...] = rc_ref[...].astype(F32).T.astype(BF16)

    @pl.when((c == 0) & last)
    def _():
        bias, alog = bias_ref[...], alog_ref[...]
        _, d, _, a = steps(pdt_ref[...], bias, alog)
        pwcat[...] = cat2(jnp.exp(a[TOK - 1 :, :] - a) * d)
        pecat[...] = cat2(jnp.broadcast_to(jnp.exp(a[TOK - 1 :, :]), (NS, NH)))
        pbt[...] = pb_ref[...].astype(F32).T.astype(BF16)

    spread = spreader(c, 2 * NH)

    def put(ref, value):
        ref[0] = value[:, :128]
        ref[1] = value[:, 128:]

    hi, lo = split2(nn(wcat[...], spread) * rx_ref[...].astype(F32))
    put(fresh_ref, nn(bt[...], hi) + nn(bt[...], lo))
    hi, lo = split2(nn(ecat[...], spread) * gy_ref[...].astype(F32))
    put(entry_ref, nn(ct[...], hi) + nn(ct[...], lo))

    @pl.when(last)
    def _():
        hi, lo = split2(nn(pwcat[...], spread) * px_ref[...].astype(F32))
        eye = jnp.where(iota((NS, NS), 0) == iota((NS, NS), 1), 1.0, 0.0).astype(BF16)
        saved = nt(eye, ps_ref[...])
        put(end_ref, nn(pecat[...], spread) * saved + (nn(pbt[...], hi) + nn(pbt[...], lo)))

    @pl.when(jnp.logical_not(last))
    def _():
        end_ref[...] = jnp.zeros_like(end_ref)


def first_call(length, rx, rb, rc, rdt, gy, px, pb, pdt, ps, bias, alog):
    wide = pl.BlockSpec((TOK, LANES), lambda c: (0, c))
    whole = lambda shape: pl.BlockSpec(shape, lambda c: (0,) * len(shape))
    state = pl.BlockSpec((2, NS, 128), lambda c: (c, 0, 0))
    shape = jax.ShapeDtypeStruct((PAIRS, NS, 128), F32)
    return pl.pallas_call(
        first_kernel,
        grid=(CHUNKS,),
        out_shape=(shape, shape, shape),
        in_specs=[
            pl.BlockSpec(memory_space=pltpu.SMEM),
            wide,
            whole((TOK, NS)),
            whole((TOK, NS)),
            whole((TOK, NH)),
            wide,
            wide,
            whole((TOK, NS)),
            whole((TOK, NH)),
            pl.BlockSpec((LANES, NS), lambda c: (c, 0)),
            whole((1, NH)),
            whole((1, NH)),
        ],
        out_specs=(state, state, state),
        scratch_shapes=[
            pltpu.VMEM((TOK, 2 * NH), BF16),
            pltpu.VMEM((TOK, 2 * NH), BF16),
            pltpu.VMEM((NS, TOK), BF16),
            pltpu.VMEM((NS, TOK), BF16),
            pltpu.VMEM((TOK, 2 * NH), BF16),
            pltpu.VMEM((NS, 2 * NH), BF16),
            pltpu.VMEM((NS, TOK), BF16),
        ],
        compiler_params=pltpu.CompilerParams(vmem_limit_bytes=LIMIT),
        name="first",
    )(length, rx, rb, rc, rdt, gy, px, pb, pdt, ps, bias, alog)


def exchange_kernel(
    nz, nx, ny,
    fresh_ref, entry_ref, end_in, decay_ref, scale_ref,
    pre_out, suf_out, seed_out, end_out,
    pre, suf, fsend, bsend, seedc, ra, rb, sa, sb, ra2, rb2, own, rz, zfull, enda, endb, endown, seed, end,
    fs, fr, bs, br, s1, r1, s2, r2, s3, r3, s4, r4, s5, r5, s6, r6, e1s, e1r, e2s, e2r, e3s, e3r,
):
    dp, z, r = lax.axis_index("dp"), lax.axis_index("ctx"), lax.axis_index("resp")
    x, y = r // ny, lax.rem(r, ny)
    half = PAIRS // 2
    pa, pb = half // nx, half // ny
    qa, qb = pa // ny, pb // nx
    rows = NS // nz
    dev = lambda zz, xx, yy: (dp, zz, xx * ny + yy)
    xs = [lax.rem(x + i, nx) for i in range(1, nx)]
    ys = [lax.rem(y + i, ny) for i in range(1, ny)]
    zs = [lax.rem(z + i, nz) for i in range(1, nz)]

    barrier = pltpu.get_barrier_semaphore()
    partners = [dev(z, t, y) for t in xs] + [dev(z, x, t) for t in ys] + [dev(t, x, y) for t in zs]
    for partner in partners:
        pl.semaphore_signal(barrier, inc=1, device_id=partner, device_id_type=MESH)

    def scale(q, carry):
        seedc[q] = entry_ref[q] * scale_ref[q]
        return carry

    lax.fori_loop(0, PAIRS, scale, 0)

    @pl.when(z == 0)
    def _():
        pre[...] = jnp.zeros_like(pre)

    @pl.when(z == nz - 1)
    def _():
        suf[...] = jnp.zeros_like(suf)

    pl.semaphore_wait(barrier, len(partners))

    def copy(src, dst, send, recv, to):
        return pltpu.make_async_remote_copy(
            src_ref=src, dst_ref=dst, send_sem=send, recv_sem=recv, device_id=to, device_id_type=MESH
        )

    def phase1():
        return [
            copy(seedc.at[pl.ds(t * pa, pa)], ra.at[i], s1.at[i], r1.at[i], dev(z, t, y))
            for i, t in enumerate(xs)
        ] + [
            copy(seedc.at[pl.ds(half + t * pb, pb)], rb.at[i], s1.at[nx + i], r1.at[nx + i], dev(z, x, t))
            for i, t in enumerate(ys)
        ]

    def phase2():
        return [
            copy(sa.at[pl.ds(t * qa, qa)], ra2.at[i], s2.at[i], r2.at[i], dev(z, x, t))
            for i, t in enumerate(ys)
        ] + [
            copy(sb.at[pl.ds(t * qb, qb)], rb2.at[i], s2.at[ny + i], r2.at[ny + i], dev(z, t, y))
            for i, t in enumerate(xs)
        ]

    def phase3():
        return [
            copy(own.at[:, pl.ds(t * rows, rows)], rz.at[i], s3.at[i], r3.at[i], dev(t, x, y))
            for i, t in enumerate(zs)
        ]

    def phase4():
        mine = zfull.at[:, pl.ds(z * rows, rows)]
        return [copy(mine, mine, s4.at[i], r4.at[i], dev(t, x, y)) for i, t in enumerate(zs)]

    la, lb = x * pa + y * qa, half + y * pb + x * qb

    def phase5():
        found = []
        for k, whole in enumerate((seed, end)):
            for i, t in enumerate(ys):
                at = k * (nx + ny) + i
                found.append(
                    copy(zfull.at[pl.ds(k * (qa + qb), qa)], whole.at[pl.ds(la, qa)], s5.at[at], r5.at[at], dev(z, x, t))
                )
            for i, t in enumerate(xs):
                at = k * (nx + ny) + ny + i
                found.append(
                    copy(zfull.at[pl.ds(k * (qa + qb) + qa, qb)], whole.at[pl.ds(lb, qb)], s5.at[at], r5.at[at], dev(z, t, y))
                )
        return found

    def phase6():
        found = []
        for k, whole in enumerate((end, seed)):
            for i, t in enumerate(xs):
                at = k * (nx + ny) + i
                mine = whole.at[pl.ds(x * pa, pa)]
                found.append(copy(mine, mine, s6.at[at], r6.at[at], dev(z, t, y)))
            for i, t in enumerate(ys):
                at = k * (nx + ny) + nx + i
                mine = whole.at[pl.ds(half + y * pb, pb)]
                found.append(copy(mine, mine, s6.at[at], r6.at[at], dev(z, x, t)))
        return found

    on_plane = z == nz - 1
    on_x, on_y = on_plane & (x == nx - 1), on_plane & (y == ny - 1)
    source = on_x & on_y

    def end1():
        return [
            copy(end_in.at[pl.ds(t * pa, pa)], enda, e1s.at[i], e1r.at[0], dev(z, t, y)) for i, t in enumerate(xs)
        ] + [
            copy(end_in.at[pl.ds(half + t * pb, pb)], endb, e1s.at[nx + i], e1r.at[1], dev(z, x, t))
            for i, t in enumerate(ys)
        ]

    def end2a():
        return [
            copy(enda.at[pl.ds(t * qa, qa)], endown.at[pl.ds(0, qa)], e2s.at[i], e2r.at[0], dev(z, x, t))
            for i, t in enumerate(ys)
        ]

    def end2b():
        return [
            copy(endb.at[pl.ds(t * qb, qb)], endown.at[pl.ds(qa, qb)], e2s.at[ny + i], e2r.at[1], dev(z, t, y))
            for i, t in enumerate(xs)
        ]

    def end3():
        return [
            copy(
                endown.at[:, pl.ds(t * rows, rows)], zfull.at[pl.ds(qa + qb, qa + qb), pl.ds(t * rows, rows)],
                e3s.at[i], e3r.at[0], dev(t, x, y),
            )
            for i, t in enumerate(zs)
        ]

    def start(copies):
        for one in copies:
            one.start()

    def wait_send(copies):
        for one in copies:
            one.wait_send()

    def wait_recv(copies):
        for one in copies:
            one.wait_recv()

    def do1():
        start(phase1())

        @pl.when(source)
        def _():
            start(end1())

    def do2():
        wait_recv(phase1())
        for q in range(pa):
            total = seedc[x * pa + q]
            for i in range(nx - 1):
                total = total + ra[i, q]
            sa[q] = total
        for q in range(pb):
            total = seedc[half + y * pb + q]
            for i in range(ny - 1):
                total = total + rb[i, q]
            sb[q] = total
        start(phase2())

        @pl.when(source)
        def _():
            enda[...] = end_in[pl.ds(x * pa, pa)]
            endb[...] = end_in[pl.ds(half + y * pb, pb)]

        @pl.when(on_y)
        def _():
            @pl.when(x != nx - 1)
            def _():
                end1()[0].wait_recv()

            start(end2a())
            for q in range(qa):
                endown[q] = enda[y * qa + q]

        @pl.when(on_x)
        def _():
            @pl.when(y != ny - 1)
            def _():
                end1()[nx - 1].wait_recv()

            start(end2b())
            for q in range(qb):
                endown[qa + q] = endb[x * qb + q]

    def do3():
        wait_recv(phase2())
        for q in range(qa):
            total = sa[y * qa + q]
            for i in range(ny - 1):
                total = total + ra2[i, q]
            own[q] = total
        for q in range(qb):
            total = sb[x * qb + q]
            for i in range(nx - 1):
                total = total + rb2[i, q]
            own[qa + q] = total
        start(phase3())

        @pl.when(on_plane)
        def _():
            @pl.when(y != ny - 1)
            def _():
                end2a()[0].wait_recv()

            @pl.when(x != nx - 1)
            def _():
                end2b()[0].wait_recv()

            start(end3())
            mine = pl.ds(z * rows, rows)
            for q in range(qa + qb):
                zfull[qa + qb + q, mine] = endown[q, mine]

    def do4():
        wait_recv(phase3())
        mine = pl.ds(z * rows, rows)
        for q in range(qa + qb):
            total = own[q, mine]
            for i in range(nz - 1):
                total = total + rz[i, q]
            zfull[q, mine] = total

        @pl.when(jnp.logical_not(on_plane))
        def _():
            end3()[0].wait_recv()

        start(phase4())

    def do5():
        wait_recv(phase4())
        start(phase5())
        for k, whole in enumerate((seed, end)):
            for q in range(qa):
                whole[la + q] = zfull[k * (qa + qb) + q]
            for q in range(qb):
                whole[lb + q] = zfull[k * (qa + qb) + qa + q]

    def do6():
        wait_recv(phase5())
        start(phase6())

    def do7():
        wait_recv(phase6())
        for phase in (phase1, phase2, phase3, phase4, phase5, phase6):
            wait_send(phase())

        @pl.when(source)
        def _():
            wait_send(end1())

        @pl.when(on_y)
        def _():
            wait_send(end2a())

        @pl.when(on_x)
        def _():
            wait_send(end2b())

        @pl.when(on_plane)
        def _():
            wait_send(end3())

    piece = 1
    count = PAIRS // piece

    def forward(c):
        at = pl.ds(c * piece, piece)
        return copy(fsend.at[at], pre.at[at], fs.at[c], fr.at[c], dev(lax.rem(z + 1, nz), x, y))

    def backward(c):
        at = pl.ds(c * piece, piece)
        return copy(bsend.at[at], suf.at[at], bs.at[c], br.at[c], dev(lax.rem(z + nz - 1, nz), x, y))

    def step(i, carry):
        cf = i - z

        @pl.when((cf >= 0) & (cf < count))
        def _():
            @pl.when(z > 0)
            def _():
                forward(cf).wait_recv()

            @pl.when(z < nz - 1)
            def _():
                at = pl.ds(cf * piece, piece)
                fsend[at] = decay_ref[at] * pre[at] + fresh_ref[at]
                forward(cf).start()

        cb = i - (nz - 1 - z)

        @pl.when((cb >= 0) & (cb < count))
        def _():
            @pl.when(z < nz - 1)
            def _():
                backward(cb).wait_recv()

            @pl.when(z > 0)
            def _():
                at = pl.ds(cb * piece, piece)
                bsend[at] = decay_ref[at] * suf[at] + entry_ref[at]
                backward(cb).start()

        return carry

    total = count + nz - 1
    do1()
    marks = [total * k // 7 for k in range(1, 6)]
    done = 0
    for mark, act in zip(marks, (do2, do3, do4, do5, do6)):
        lax.fori_loop(done, mark, step, 0)
        act()
        done = mark
    lax.fori_loop(done, total, step, 0)
    do7()

    def finish(c, carry):
        @pl.when(z < nz - 1)
        def _():
            forward(c).wait_send()

        @pl.when(z > 0)
        def _():
            backward(c).wait_send()

        return carry

    lax.fori_loop(0, count, finish, 0)
    pre_out[...] = pre[...]
    suf_out[...] = suf[...]
    seed_out[...] = seed[...]
    end_out[...] = end[...]


def factors(count):
    first = 1
    while first * first < count:
        first *= 2
    return first, count // first


def exchange_call(mesh_shape, fresh, entry, end, decay, scale):
    nz = mesh_shape["ctx"]
    nx, ny = factors(mesh_shape["resp"])
    half = PAIRS // 2
    pa, pb = half // nx, half // ny
    qa, qb = pa // ny, pb // nx
    rows = NS // nz
    shape = jax.ShapeDtypeStruct((PAIRS, NS, 128), F32)
    vmem = pl.BlockSpec(memory_space=pltpu.VMEM)
    buf = lambda *lead: pltpu.VMEM(lead + (128,), F32)
    sem = lambda n: pltpu.SemaphoreType.DMA((n,))
    return pl.pallas_call(
        functools.partial(exchange_kernel, nz, nx, ny),
        out_shape=(shape,) * 4,
        in_specs=[vmem] * 5,
        out_specs=(vmem,) * 4,
        scratch_shapes=[buf(PAIRS, NS)] * 5
        + [
            buf(nx - 1, pa, NS),
            buf(ny - 1, pb, NS),
            buf(pa, NS),
            buf(pb, NS),
            buf(ny - 1, qa, NS),
            buf(nx - 1, qb, NS),
            buf(qa + qb, NS),
            buf(nz - 1, qa + qb, rows),
            buf(2 * (qa + qb), NS),
            buf(pa, NS),
            buf(pb, NS),
            buf(qa + qb, NS),
            buf(PAIRS, NS),
            buf(PAIRS, NS),
        ]
        + [sem(PAIRS)] * 4
        + [sem(nx + ny)] * 4
        + [sem(nz)] * 4
        + [sem(2 * (nx + ny))] * 4
        + [sem(nx + ny), sem(2), sem(nx + ny), sem(2), sem(nz), sem(1)],
        compiler_params=pltpu.CompilerParams(collective_id=0, has_side_effects=True, vmem_limit_bytes=LIMIT),
        name="exchange",
    )(fresh, entry, end, decay, scale)


def last_kernel(
    len_ref, fac_ref, rx_ref, rb_ref, rc_ref, rdt_ref, gy_ref, px_ref, pb_ref, pdt_ref, ps_ref, bias_ref, alog_ref,
    skip_ref, pre_ref, suf_ref, end_ref, seed_ref, scan_ref, follow_ref,
    pdx_ref, pdb_ref, pdd_ref, rdx_ref, rdb_ref, rdc_ref, rdd_ref, small_ref,
    a_ch, d_ch, a_t, gt, dgt, dcat, wcat, ecat, e_in, r_in, d_in, z_in, row, acc1, acc2, acc3, inner, outer,
    pwcat, pr, pd, pz, pacc, pinner,
):
    c = pl.program_id(0)
    mask = row_mask(len_ref)

    @pl.when(c == 0)
    def _():
        bias, alog = bias_ref[...], alog_ref[...]
        z, d, _, a = steps(rdt_ref[...], bias, alog)
        z_in[...] = z
        d_in[...] = d
        at = a.T
        for k in range(CHUNKS):
            a_ch[k] = a[:, k * PER : k * PER + PER]
            d_ch[k] = d[:, k * PER : k * PER + PER]
            a_t[k] = at[k * PER : k * PER + PER]
        e = jnp.exp(a)
        r = jnp.exp(a[TOK - 1 :, :] - a)
        e_in[...] = e
        r_in[...] = r
        dcat[...] = cat2(d)
        wcat[...] = cat2(r * d)
        ecat[...] = cat2(e)
        scores = nt(rb_ref[...], rc_ref[...])
        gt[...] = jnp.where(iota((TOK, TOK), 0) <= iota((TOK, TOK), 1), scores, 0.0)
        dgt[...] = jnp.zeros_like(dgt)
        for acc in (acc1, acc2, acc3, inner, outer, pacc, pinner, rdb_ref, rdc_ref, pdb_ref):
            acc[...] = jnp.zeros_like(acc)
        z, d, _, a = steps(pdt_ref[...], bias, alog)
        pz[...] = z
        pd[...] = d
        r = jnp.exp(a[TOK - 1 :, :] - a)
        pr[...] = r
        pwcat[...] = cat2(r * d)

    spread2 = spreader(c, 2 * NH)
    spread = spread2[:NH]
    both = lambda ref: jnp.concatenate([ref[0], ref[1]], axis=1)

    x = rx_ref[...]
    gy = (gy_ref[...].astype(F32) * mask).astype(BF16)
    xf, gf = x.astype(F32), gy.astype(F32)
    lane = iota((1, 128), 1) < HD
    q1 = []
    for pair in range(2):
        xp, gp = x[:, pair * 128 : pair * 128 + 128], gy[:, pair * 128 : pair * 128 + 128]
        total = [None] * 4
        for odd in range(2):
            j = 2 * pair + odd
            own = jnp.logical_not(lane) if odd else lane
            xh = jnp.where(own, xp, jnp.zeros_like(xp))
            gh = jnp.where(own, gp, jnp.zeros_like(gp))
            col, dcol, arow = a_ch[c, :, j : j + 1], d_ch[c, :, j : j + 1], a_t[c, j : j + 1, :]
            rows = [None, None]
            for b in range(4):
                s0 = b * 64
                t0 = (b // 2) * 128
                sl = slice(s0, s0 + 64)
                g = gt[sl, t0:]
                decay = jnp.exp(jnp.minimum(arow[:, t0:] - col[sl], 0.0))
                hi, lo = split2(decay * g)
                gpart = gh[t0:]
                q = nn(hi, gpart) + nn(lo, gpart)
                total[b] = q if total[b] is None else total[b] + q
                k = decay * nt(xh[sl], gpart) * dcol[sl]
                dgt[sl, t0:] += k
                part = jnp.sum(k * g, axis=0, keepdims=True)
                at = b // 2
                rows[at] = part if rows[at] is None else rows[at] + part
            row[c, j : j + 1, :] = rows[0]
            row[c, j : j + 1, 128:] += rows[1]
        q1.append(jnp.concatenate(total, axis=0))
    q1 = jnp.concatenate(q1, axis=1)
    factor = fac_ref[0, 0]
    state = scan_ref[0] * both(end_ref) + both(pre_ref)
    grad = both(suf_ref)
    shi, slo = split2(state)
    ghi, glo = split2(grad)
    rb, rc = rb_ref[...], rc_ref[...]
    q2 = nn(rb, ghi) + nn(rb, glo)
    cs = nn(rc, shi) + nn(rc, slo)
    wide_w = nn(wcat[...], spread2)
    rdx_ref[...] = (factor * (nn(dcat[...], spread2) * q1 + wide_w * q2 + skip_ref[0] * gf)).astype(BF16)
    acc1[...] += by_head(xf * q1, spread)
    acc2[...] += by_head(xf * q2, spread)
    acc3[...] += by_head(gf * cs, spread)
    whi, wlo = split2(wide_w * xf)
    rdb_ref[...] += nt(whi, ghi) + (nt(wlo, ghi) + nt(whi, glo))
    ehi, elo = split2(nn(ecat[...], spread2) * gf)
    rdc_ref[...] += nt(ehi, shi) + (nt(elo, shi) + nt(ehi, slo))
    inner[...] += by_head(fold8(state * grad), spread)
    outer[...] += by_head(fold8(xf * gf), spread)

    pxf = px_ref[...].astype(F32)
    pgrad = follow_ref[0] * both(seed_ref)
    ghi, glo = split2(pgrad)
    pb = pb_ref[...]
    q2 = nn(pb, ghi) + nn(pb, glo)
    wide_w = nn(pwcat[...], spread2)
    pdx_ref[...] = (wide_w * q2).astype(BF16)
    pacc[...] += by_head(pxf * q2, spread)
    whi, wlo = split2(wide_w * pxf)
    pdb_ref[...] += nt(whi, ghi) + (nt(wlo, ghi) + nt(whi, glo))
    eye = jnp.where(iota((NS, NS), 0) == iota((NS, NS), 1), 1.0, 0.0).astype(BF16)
    pinner[...] += by_head(fold8(nt(eye, ps_ref[...]) * pgrad), spread)

    @pl.when(c == CHUNKS - 1)
    def _():
        rate = -jnp.exp(alog_ref[...])

        def close(z, d, r, dstep, da, last):
            cum = exact_nn(upper(), da) + last
            ddt = (dstep + rate * cum) / (1.0 + jnp.exp(-z))
            return ddt, cum * (rate * d)

        column = lambda v: jnp.sum(v, axis=0, keepdims=True)
        d, r, e = d_in[...], r_in[...], e_in[...]
        dstep = acc1[...] + r * acc2[...]
        erow = jnp.concatenate([row[k] for k in range(CHUNKS)], axis=0).T
        da = erow + e * acc3[...] - d * dstep
        last = e[TOK - 1 :] * column(inner[...]) + column(r * d * acc2[...])
        ddt, dalog = close(z_in[...], d, r, dstep, da, last)
        ddt = factor * ddt
        rdd_ref[...] = ddt
        bias_sum, alog_sum = column(ddt), factor * column(dalog)
        skip_sum = factor * column(outer[...])
        keep = jnp.where(iota((TOK, TOK), 0) <= iota((TOK, TOK), 1), dgt[...], 0.0)
        hi, lo = split2(keep)
        rdb_ref[...] = factor * (rdb_ref[...] + (nn(hi, rc) + nn(lo, rc)))
        hi, lo = split2(keep.T)
        rdc_ref[...] = factor * (rdc_ref[...] + (nn(hi, rb) + nn(lo, rb)))

        d, r = pd[...], pr[...]
        dstep = r * pacc[...]
        weighted = d * dstep
        last_decay = jnp.exp(column(rate * d))
        last = last_decay * column(pinner[...]) + column(weighted)
        ddt, dalog = close(pz[...], d, r, dstep, -weighted, last)
        pdd_ref[...] = ddt
        small_ref[0:1] = bias_sum + column(ddt)
        small_ref[1:2] = alog_sum + column(dalog)
        small_ref[2:3] = skip_sum


def last_call(length, factor, rx, rb, rc, rdt, gy, px, pb, pdt, ps, bias, alog, skip, pre, suf, end, seed, scan, follow):
    wide = pl.BlockSpec((TOK, LANES), lambda c: (0, c))
    whole = lambda *shape: pl.BlockSpec(shape, lambda c: (0,) * len(shape))
    state = pl.BlockSpec((2, NS, 128), lambda c: (c, 0, 0))
    lanes = pl.BlockSpec((1, 1, LANES), lambda c: (c, 0, 0))
    smem = pl.BlockSpec(memory_space=pltpu.SMEM)
    out = jax.ShapeDtypeStruct
    v = lambda *shape: pltpu.VMEM(shape, F32)
    b = lambda *shape: pltpu.VMEM(shape, BF16)
    return pl.pallas_call(
        last_kernel,
        grid=(CHUNKS,),
        out_shape=(
            out((TOK, NH * HD), BF16),
            out((TOK, NS), F32),
            out((TOK, NH), F32),
            out((TOK, NH * HD), BF16),
            out((TOK, NS), F32),
            out((TOK, NS), F32),
            out((TOK, NH), F32),
            out((3, NH), F32),
        ),
        in_specs=[
            smem, smem, wide, whole(TOK, NS), whole(TOK, NS), whole(TOK, NH), wide, wide, whole(TOK, NS), whole(TOK, NH),
            pl.BlockSpec((LANES, NS), lambda c: (c, 0)), whole(1, NH), whole(1, NH), lanes,
            state, state, state, state, lanes, lanes,
        ],
        out_specs=(
            wide, whole(TOK, NS), whole(TOK, NH), wide, whole(TOK, NS), whole(TOK, NS), whole(TOK, NH), whole(3, NH),
        ),
        scratch_shapes=[
            v(CHUNKS, TOK, PER), v(CHUNKS, TOK, PER), v(CHUNKS, PER, TOK), v(TOK, TOK), v(TOK, TOK),
            b(TOK, 2 * NH), b(TOK, 2 * NH), b(TOK, 2 * NH),
            v(TOK, NH), v(TOK, NH), v(TOK, NH), v(TOK, NH), v(CHUNKS, PER, TOK),
            v(TOK, NH), v(TOK, NH), v(TOK, NH), v(8, NH), v(8, NH),
            b(TOK, 2 * NH), v(TOK, NH), v(TOK, NH), v(TOK, NH), v(TOK, NH), v(8, NH),
        ],
        compiler_params=pltpu.CompilerParams(vmem_limit_bytes=LIMIT),
        name="last",
    )(length, factor, rx, rb, rc, rdt, gy, px, pb, pdt, ps, bias, alog, skip, pre, suf, end, seed, scan, follow)


def body(
    mesh_shape,
    prompt_x, prompt_b, prompt_dt, prompt_states, resp_x, resp_b, resp_c, resp_dt, grad_out, lengths, advantages,
    dt_bias, a_log, skip,
):
    nz, nr = mesh_shape["ctx"], mesh_shape["resp"]
    px, pb, pdt = prompt_x[0], prompt_b[0], prompt_dt[0]
    ps = prompt_states.reshape(NH * HD, NS)
    rx, rb, rc, rdt, gy = resp_x[0, 0], resp_b[0, 0], resp_c[0, 0], resp_dt[0, 0], grad_out[0, 0]
    bias, alog = dt_bias[None], a_log[None]

    def block_decay(dt):
        return jnp.exp(jnp.sum(-jnp.exp(alog) * jax.nn.softplus(dt + bias), axis=0))

    own_decay = block_decay(rdt)
    decays = jnp.stack([own_decay, block_decay(pdt)])
    every = lax.all_gather(decays, ("ctx", "resp"))
    here, row = lax.axis_index("ctx"), lax.axis_index("resp")
    of_resp = lax.dynamic_index_in_dim(every[:, 0].reshape(nz, nr, NH), row, 1, keepdims=False)
    scan = jnp.prod(jnp.where((jnp.arange(nz) < here)[:, None], of_resp, 1.0), axis=0)
    later = (jnp.arange(nz * nr) > here * nr + row)[:, None]
    follow = jnp.prod(jnp.where(later, every[:, 1], 1.0), axis=0)
    length = lengths
    factor = advantages * float(nz * TOK) / lengths.astype(F32)

    lanes = lambda v: jnp.repeat(v, HD).reshape(CHUNKS, 1, LANES)
    pairs = lambda v: jnp.repeat(v, HD).reshape(PAIRS, 1, 128)

    fresh, entry, end = first_call(length, rx, rb, rc, rdt, gy, px, pb, pdt, ps, bias, alog)
    pre, suf, seed, end = exchange_call(
        mesh_shape, fresh, entry, end, pairs(own_decay), pairs(scan * factor[0, 0])
    )
    pdx, pdb, pdd, rdx, rdb, rdc, rdd, small = last_call(
        length, factor, rx, rb, rc, rdt, gy, px, pb, pdt, ps, bias, alog, lanes(skip),
        pre, suf, end, seed, lanes(scan), lanes(follow),
    )
    small = lax.psum(small, ("dp", "ctx", "resp"))
    return (
        pdx[None], pdb[None], pdd[None], rdx[None, None], rdb[None, None], rdc[None, None], rdd[None, None],
        small[0], small[1], small[2],
    )


def solution(mesh):
    wide = P("dp", ("ctx", "resp"), None)
    long = P("dp", "resp", "ctx", None)
    in_specs = (
        wide, wide, wide, P("dp", ("ctx", "resp"), None, None, None), long, long, long, long, long,
        P("dp", "resp"), P("dp", "resp"), P(), P(), P(),
    )
    out_specs = (wide, wide, wide, long, long, long, long, P(), P(), P())
    return jax.shard_map(
        functools.partial(body, dict(mesh.shape)), mesh=mesh, in_specs=in_specs, out_specs=out_specs, check_vma=False
    )
```

```python
import functools

import jax
import jax.numpy as jnp
from jax import lax
from jax.experimental import pallas as pl
from jax.experimental.pallas import tpu as pltpu
from jax.sharding import PartitionSpec as P

MESH = pl.DeviceIdType.MESH
F32 = jnp.float32
BF16 = jnp.bfloat16
TOK = 256
LANES = 256
PER = 4
NH = 64
HD = 64
NS = 128
CHUNKS = 16
PAIRS = 32
LIMIT = 56 * 1024 * 1024


def nn(a, b):
    return lax.dot_general(a, b, (((1,), (0,)), ((), ())), preferred_element_type=F32)


def nt(a, b):
    return lax.dot_general(a, b, (((1,), (1,)), ((), ())), preferred_element_type=F32)


def split2(v):
    hi = v.astype(BF16)
    return hi, (v - hi.astype(F32)).astype(BF16)


def split3(v):
    hi = v.astype(BF16)
    rest = v - hi.astype(F32)
    mid = rest.astype(BF16)
    return hi, mid, (rest - mid.astype(F32)).astype(BF16)


def exact_nn(tri, v):
    hi, mid, lo = split3(v)
    return nn(tri, hi) + (nn(tri, mid) + nn(tri, lo))


def iota(shape, dim):
    return lax.broadcasted_iota(jnp.int32, shape, dim)


def lower():
    return jnp.where(iota((TOK, TOK), 0) >= iota((TOK, TOK), 1), 1.0, 0.0).astype(BF16)


def upper():
    return jnp.where(iota((TOK, TOK), 0) <= iota((TOK, TOK), 1), 1.0, 0.0).astype(BF16)


def spreader(c, rows):
    head = iota((rows, LANES), 0) & (NH - 1)
    lane = iota((rows, LANES), 1) >> 6
    return jnp.where(head == lane + c * PER, 1.0, 0.0).astype(BF16)


def steps(dt, bias, alog):
    z = dt + bias
    d = jnp.maximum(z, 0.0) + jnp.log1p(jnp.exp(-jnp.abs(z)))
    rate = -jnp.exp(alog)
    a = exact_nn(lower(), rate * d)
    return z, d, rate, a


def cat2(v):
    hi, lo = split2(v)
    return jnp.concatenate([hi, lo], axis=1)


def by_head(v, spread):
    hi, lo = split2(v)
    return nt(hi, spread) + nt(lo, spread)


def fold8(v):
    total = v[0:8]
    for at in range(8, v.shape[0], 8):
        total = total + v[at : at + 8]
    return total


def cat3(v):
    return jnp.concatenate(split3(v), axis=1)


def column(v):
    return jnp.sum(v, axis=0, keepdims=True)


def triangle():
    return iota((TOK, TOK), 0) <= iota((TOK, TOK), 1)


def both(ref, c):
    return jnp.concatenate([ref[2 * c], ref[2 * c + 1]], axis=1)


def row_mask(length_ref):
    position = lax.axis_index("ctx") * TOK + iota((TOK, 1), 0)
    return jnp.where(position < length_ref[0, 0], 1.0, 0.0)


def first_kernel(
    len_ref, rx_ref, rb_ref, rc_ref, rdt_ref, gy_ref, px_ref, pb_ref, pdt_ref, ps_ref, bias_ref, alog_ref,
    fresh_ref, entry_ref, end_ref, decay_ref,
    wcat, ecat, bt, ct, pwcat, pecat, pbt,
):
    c = pl.program_id(0)
    last = (lax.axis_index("ctx") == lax.axis_size("ctx") - 1) & (
        lax.axis_index("resp") == lax.axis_size("resp") - 1
    )

    @pl.when(c == 0)
    def _():
        bias, alog = bias_ref[...], alog_ref[...]
        _, d, _, a = steps(rdt_ref[...], bias, alog)
        wcat[...] = cat2(jnp.exp(a[TOK - 1 :, :] - a) * d)
        ecat[...] = cat2(jnp.exp(a) * row_mask(len_ref))
        bt[...] = rb_ref[...].astype(F32).T.astype(BF16)
        ct[...] = rc_ref[...].astype(F32).T.astype(BF16)
        decay_ref[...] = jnp.ones_like(decay_ref)
        decay_ref[0:1, :NH] = jnp.exp(a[TOK - 1 :, :])
        _, _, _, a = steps(pdt_ref[...], bias, alog)
        decay_ref[1:2, :NH] = jnp.exp(a[TOK - 1 :, :])

    @pl.when((c == 0) & last)
    def _():
        bias, alog = bias_ref[...], alog_ref[...]
        _, d, _, a = steps(pdt_ref[...], bias, alog)
        pwcat[...] = cat2(jnp.exp(a[TOK - 1 :, :] - a) * d)
        pecat[...] = cat2(jnp.broadcast_to(jnp.exp(a[TOK - 1 :, :]), (NS, NH)))
        pbt[...] = pb_ref[...].astype(F32).T.astype(BF16)

    spread = spreader(c, 2 * NH)

    def put(ref, value):
        ref[0] = value[:, :128]
        ref[1] = value[:, 128:]

    hi, lo = split2(nn(wcat[...], spread) * rx_ref[...].astype(F32))
    put(fresh_ref, nn(bt[...], hi) + nn(bt[...], lo))
    hi, lo = split2(nn(ecat[...], spread) * gy_ref[...].astype(F32))
    put(entry_ref, nn(ct[...], hi) + nn(ct[...], lo))

    @pl.when(last)
    def _():
        hi, lo = split2(nn(pwcat[...], spread) * px_ref[...].astype(F32))
        eye = jnp.where(iota((NS, NS), 0) == iota((NS, NS), 1), 1.0, 0.0).astype(BF16)
        saved = nt(eye, ps_ref[...])
        put(end_ref, nn(pecat[...], spread) * saved + (nn(pbt[...], hi) + nn(pbt[...], lo)))

    @pl.when(jnp.logical_not(last))
    def _():
        end_ref[...] = jnp.zeros_like(end_ref)


def first_call(length, rx, rb, rc, rdt, gy, px, pb, pdt, ps, bias, alog):
    wide = pl.BlockSpec((TOK, LANES), lambda c: (0, c))
    whole = lambda shape: pl.BlockSpec(shape, lambda c: (0,) * len(shape))
    state = pl.BlockSpec((2, NS, 128), lambda c: (c, 0, 0))
    shape = jax.ShapeDtypeStruct((PAIRS, NS, 128), F32)
    return pl.pallas_call(
        first_kernel,
        grid=(CHUNKS,),
        out_shape=(shape, shape, shape, jax.ShapeDtypeStruct((8, 128), F32)),
        in_specs=[
            pl.BlockSpec(memory_space=pltpu.SMEM),
            wide,
            whole((TOK, NS)),
            whole((TOK, NS)),
            whole((TOK, NH)),
            wide,
            wide,
            whole((TOK, NS)),
            whole((TOK, NH)),
            pl.BlockSpec((LANES, NS), lambda c: (c, 0)),
            whole((1, NH)),
            whole((1, NH)),
        ],
        out_specs=(state, state, state, whole((8, 128))),
        scratch_shapes=[
            pltpu.VMEM((TOK, 2 * NH), BF16),
            pltpu.VMEM((TOK, 2 * NH), BF16),
            pltpu.VMEM((NS, TOK), BF16),
            pltpu.VMEM((NS, TOK), BF16),
            pltpu.VMEM((TOK, 2 * NH), BF16),
            pltpu.VMEM((NS, 2 * NH), BF16),
            pltpu.VMEM((NS, TOK), BF16),
        ],
        compiler_params=pltpu.CompilerParams(vmem_limit_bytes=LIMIT),
        name="first",
    )(length, rx, rb, rc, rdt, gy, px, pb, pdt, ps, bias, alog)


LAG = 3
MARKS = (1, 6, 8, 10, 13, 16)


def main_kernel(
    nz, nx, ny,
    len_ref, fac_ref, fresh_ref, entry_ref, end_in, tile_ref,
    rx_ref, rb_ref, rc_ref, rdt_ref, gy_ref, px_ref, pb_ref, pdt_ref, ps_ref, bias_ref, alog_ref, skip_ref,
    pdx_ref, pdb_ref, pdd_ref, rdx_ref, rdb_ref, rdc_ref, rdd_ref, small_ref,
    a_ch, d_ch, a_t, gt, dgt, q1_ref, dcat, wcat, ecat, e_in, r_in, d_in, z_in, row, acc1, acc2, acc3, inner, outer,
    pwcat, pr, pd, pz, pacc, pinner, scan_ref, fol_ref, lanes_ref,
    pre, suf, fsend, bsend, seedc, seed, end, ra, rb, sa, sb, ra2, rb2, own, rz, zfull, enda, endb, endown,
    tz, ty, tx, tp, mine_y, mine_x, sx, sy, sz, sd, terms,
    fs, fr, bs, br, s1, r1, s2, r2, s3, r3, s4, r4, s5, r5, s6, r6, e1s, e1r, e2s, e2r, e3s, e3r,
    tzs, tzr, tys, tyr, txs, txr, tps, tpr, xs_s, xs_r, ys_s, ys_r, zs_s, zs_r, ds_s, ds_r,
):
    dp, z, r = lax.axis_index("dp"), lax.axis_index("ctx"), lax.axis_index("resp")
    ndp = lax.axis_size("dp")
    x, y = r // ny, lax.rem(r, ny)
    half = PAIRS // 2
    pa, pb = half // nx, half // ny
    qa, qb = pa // ny, pb // nx
    rows = NS // nz
    dev = lambda zz, xx, yy: (dp, zz, xx * ny + yy)
    xs = [lax.rem(x + i, nx) for i in range(1, nx)]
    ys = [lax.rem(y + i, ny) for i in range(1, ny)]
    zs = [lax.rem(z + i, nz) for i in range(1, nz)]
    ds = [(lax.rem(dp + i, ndp), z, r) for i in range(1, ndp)]
    factor = fac_ref[0, 0]

    barrier = pltpu.get_barrier_semaphore()
    partners = [dev(z, t, y) for t in xs] + [dev(z, x, t) for t in ys] + [dev(t, x, y) for t in zs] + ds
    for partner in partners:
        pl.semaphore_signal(barrier, inc=1, device_id=partner, device_id_type=MESH)

    bias, alog = bias_ref[...], alog_ref[...]

    def prepare():
        zz, d, _, a = steps(rdt_ref[...], bias, alog)
        z_in[...] = zz
        d_in[...] = d
        at = a.T
        for k in range(CHUNKS):
            a_ch[k] = a[:, k * PER : k * PER + PER]
            d_ch[k] = d[:, k * PER : k * PER + PER]
            a_t[k] = at[k * PER : k * PER + PER]
        e = jnp.exp(a)
        rr = jnp.exp(a[TOK - 1 :, :] - a)
        e_in[...] = e
        r_in[...] = rr
        dcat[...] = cat2(d)
        wcat[...] = cat2(rr * d)
        ecat[...] = cat2(e)
        scores = nt(rb_ref[...], rc_ref[...])
        gt[...] = jnp.where(triangle(), scores, 0.0)
        dgt[...] = jnp.zeros_like(dgt)
        for acc in (acc1, acc2, acc3, inner, outer, pacc, pinner, rdb_ref, rdc_ref, pdb_ref):
            acc[...] = jnp.zeros_like(acc)
        zz, d, _, a = steps(pdt_ref[...], bias, alog)
        pz[...] = zz
        pd[...] = d
        rr = jnp.exp(a[TOK - 1 :, :] - a)
        pr[...] = rr
        pwcat[...] = cat2(rr * d)

    def to_lanes(v, c):
        return nn(cat3(v), spreader(c, 3 * NH))

    def put_lanes(v):
        def one(c, carry):
            wide = to_lanes(v, c)
            lanes_ref[2 * c] = wide[:, :128]
            lanes_ref[2 * c + 1] = wide[:, 128:]
            return carry

        lax.fori_loop(0, CHUNKS, one, 0)

    put_lanes(tile_ref[:, :NH])

    @pl.when(z == 0)
    def _():
        pre[...] = jnp.zeros_like(pre)

    @pl.when(z == nz - 1)
    def _():
        suf[...] = jnp.zeros_like(suf)

    pl.semaphore_wait(barrier, len(partners))

    def copy(src, dst, send, recv, to):
        return pltpu.make_async_remote_copy(
            src_ref=src, dst_ref=dst, send_sem=send, recv_sem=recv, device_id=to, device_id_type=MESH
        )

    def start(copies):
        for one in copies:
            one.start()

    def wait_send(copies):
        for one in copies:
            one.wait_send()

    def wait_recv(copies):
        for one in copies:
            one.wait_recv()

    def tiles_z():
        return [copy(tile_ref, tz.at[i], tzs.at[i], tzr.at[i], dev(t, x, y)) for i, t in enumerate(zs)]

    def tiles_y():
        return [copy(tile_ref, ty.at[i], tys.at[i], tyr.at[i], dev(z, x, t)) for i, t in enumerate(ys)]

    def tiles_x():
        return [copy(mine_y, tx.at[i], txs.at[i], txr.at[i], dev(z, t, y)) for i, t in enumerate(xs)]

    def tiles_p():
        return [copy(mine_x, tp.at[i], tps.at[i], tpr.at[i], dev(t, x, y)) for i, t in enumerate(zs)]

    def before(slots, at, size):
        total = jnp.ones((8, 128), F32)
        for i in range(size - 1):
            total = total * jnp.where(i + 1 <= at, slots[i], 1.0)
        return total

    def after(slots, at, size):
        total = jnp.ones((8, 128), F32)
        for i in range(size - 1):
            total = total * jnp.where(i + 1 > at, slots[i], 1.0)
        return total

    def phase1():
        return [
            copy(seedc.at[pl.ds(t * pa, pa)], ra.at[i], s1.at[i], r1.at[i], dev(z, t, y))
            for i, t in enumerate(xs)
        ] + [
            copy(seedc.at[pl.ds(half + t * pb, pb)], rb.at[i], s1.at[nx + i], r1.at[nx + i], dev(z, x, t))
            for i, t in enumerate(ys)
        ]

    def phase2():
        return [
            copy(sa.at[pl.ds(t * qa, qa)], ra2.at[i], s2.at[i], r2.at[i], dev(z, x, t))
            for i, t in enumerate(ys)
        ] + [
            copy(sb.at[pl.ds(t * qb, qb)], rb2.at[i], s2.at[ny + i], r2.at[ny + i], dev(z, t, y))
            for i, t in enumerate(xs)
        ]

    def phase3():
        return [
            copy(own.at[:, pl.ds(t * rows, rows)], rz.at[i], s3.at[i], r3.at[i], dev(t, x, y))
            for i, t in enumerate(zs)
        ]

    def phase4():
        mine = zfull.at[:, pl.ds(z * rows, rows)]
        return [copy(mine, mine, s4.at[i], r4.at[i], dev(t, x, y)) for i, t in enumerate(zs)]

    la, lb = x * pa + y * qa, half + y * pb + x * qb

    def phase5():
        found = []
        for k, whole in enumerate((seed, end)):
            for i, t in enumerate(ys):
                at = k * (nx + ny) + i
                found.append(
                    copy(zfull.at[pl.ds(k * (qa + qb), qa)], whole.at[pl.ds(la, qa)], s5.at[at], r5.at[at], dev(z, x, t))
                )
            for i, t in enumerate(xs):
                at = k * (nx + ny) + ny + i
                found.append(
                    copy(zfull.at[pl.ds(k * (qa + qb) + qa, qb)], whole.at[pl.ds(lb, qb)], s5.at[at], r5.at[at], dev(z, t, y))
                )
        return found

    def phase6():
        found = []
        for k, whole in enumerate((end, seed)):
            for i, t in enumerate(xs):
                at = k * (nx + ny) + i
                mine = whole.at[pl.ds(x * pa, pa)]
                found.append(copy(mine, mine, s6.at[at], r6.at[at], dev(z, t, y)))
            for i, t in enumerate(ys):
                at = k * (nx + ny) + nx + i
                mine = whole.at[pl.ds(half + y * pb, pb)]
                found.append(copy(mine, mine, s6.at[at], r6.at[at], dev(z, x, t)))
        return found

    on_plane = z == nz - 1
    on_x, on_y = on_plane & (x == nx - 1), on_plane & (y == ny - 1)
    source = on_x & on_y

    def end1a(i, t):
        return copy(end_in.at[pl.ds(t * pa, pa)], enda, e1s.at[i], e1r.at[0], dev(z, t, y))

    def end1b(i, t):
        return copy(end_in.at[pl.ds(half + t * pb, pb)], endb, e1s.at[nx + i], e1r.at[1], dev(z, x, t))

    def end1():
        return [end1a(i, t) for i, t in enumerate(xs)] + [end1b(i, t) for i, t in enumerate(ys)]

    def end2a(i, t):
        return copy(enda.at[pl.ds(t * qa, qa)], endown.at[pl.ds(0, qa)], e2s.at[i], e2r.at[0], dev(z, x, t))

    def end2b(i, t):
        return copy(endb.at[pl.ds(t * qb, qb)], endown.at[pl.ds(qa, qb)], e2s.at[ny + i], e2r.at[1], dev(z, t, y))

    def end3(i, t):
        at = pl.ds(t * rows, rows)
        return copy(
            endown.at[:, at], zfull.at[pl.ds(qa + qb, qa + qb), at], e3s.at[i], e3r.at[0], dev(t, x, y)
        )

    def each(make, targets):
        return [make(i, t) for i, t in enumerate(targets)]

    def do1():
        wait_recv(tiles_z())
        wait_recv(tiles_y())
        scan = before(tz, z, nz)
        scan_ref[...] = scan
        put_lanes(scan[:, :NH] * factor)

        def scale(q, carry):
            seedc[q] = entry_ref[q] * lanes_ref[q, 0:1]
            return carry

        lax.fori_loop(0, PAIRS, scale, 0)
        start(phase1())
        put_lanes(tile_ref[:, :NH])
        fol_ref[...] = after(ty, y, ny)
        total = tile_ref[...]
        for i in range(ny - 1):
            total = total * ty[i]
        mine_y[...] = total
        start(tiles_x())

        @pl.when(source)
        def _():
            start(end1())

    def do2():
        wait_recv(phase1())
        for q in range(pa):
            total = seedc[x * pa + q]
            for i in range(nx - 1):
                total = total + ra[i, q]
            sa[q] = total
        for q in range(pb):
            total = seedc[half + y * pb + q]
            for i in range(ny - 1):
                total = total + rb[i, q]
            sb[q] = total
        start(phase2())
        wait_recv(tiles_x())
        fol_ref[...] = fol_ref[...] * after(tx, x, nx)
        total = mine_y[...]
        for i in range(nx - 1):
            total = total * tx[i]
        mine_x[...] = total
        start(tiles_p())

        @pl.when(source)
        def _():
            enda[...] = end_in[pl.ds(x * pa, pa)]
            endb[...] = end_in[pl.ds(half + y * pb, pb)]

        @pl.when(on_y)
        def _():
            @pl.when(x != nx - 1)
            def _():
                end1a(0, xs[0]).wait_recv()

            start(each(end2a, ys))
            for q in range(qa):
                endown[q] = enda[y * qa + q]

        @pl.when(on_x)
        def _():
            @pl.when(y != ny - 1)
            def _():
                end1b(0, ys[0]).wait_recv()

            start(each(end2b, xs))
            for q in range(qb):
                endown[qa + q] = endb[x * qb + q]

    def do3():
        wait_recv(phase2())
        for q in range(qa):
            total = sa[y * qa + q]
            for i in range(ny - 1):
                total = total + ra2[i, q]
            own[q] = total
        for q in range(qb):
            total = sb[x * qb + q]
            for i in range(nx - 1):
                total = total + rb2[i, q]
            own[qa + q] = total
        start(phase3())

        @pl.when(on_plane)
        def _():
            @pl.when(y != ny - 1)
            def _():
                end2a(0, ys[0]).wait_recv()

            @pl.when(x != nx - 1)
            def _():
                end2b(0, xs[0]).wait_recv()

            start(each(end3, zs))
            mine = pl.ds(z * rows, rows)
            for q in range(qa + qb):
                zfull[qa + qb + q, mine] = endown[q, mine]

    def do4():
        wait_recv(phase3())
        mine = pl.ds(z * rows, rows)
        for q in range(qa + qb):
            total = own[q, mine]
            for i in range(nz - 1):
                total = total + rz[i, q]
            zfull[q, mine] = total

        @pl.when(jnp.logical_not(on_plane))
        def _():
            end3(0, zs[0]).wait_recv()

        start(phase4())
        wait_recv(tiles_p())
        fol_ref[...] = fol_ref[...] * after(tp, z, nz)

    def do5():
        wait_recv(phase4())
        start(phase5())
        for k, whole in enumerate((seed, end)):
            for q in range(qa):
                whole[la + q] = zfull[k * (qa + qb) + q]
            for q in range(qb):
                whole[lb + q] = zfull[k * (qa + qb) + qa + q]

    def do6():
        wait_recv(phase5())
        start(phase6())

    def do7():
        wait_recv(phase6())

    def drain():
        for phase in (phase1, phase2, phase3, phase4, phase5, phase6, tiles_z, tiles_y, tiles_x, tiles_p):
            wait_send(phase())

        @pl.when(source)
        def _():
            wait_send(end1())

        @pl.when(on_y)
        def _():
            wait_send(each(end2a, ys))

        @pl.when(on_x)
        def _():
            wait_send(each(end2b, xs))

        @pl.when(on_plane)
        def _():
            wait_send(each(end3, zs))

        def finish(q, carry):
            @pl.when(z < nz - 1)
            def _():
                forward(q).wait_send()

            @pl.when(z > 0)
            def _():
                backward(q).wait_send()

            return carry

        lax.fori_loop(0, PAIRS, finish, 0)

    def forward(q):
        return copy(fsend.at[q], pre.at[q], fs.at[q], fr.at[q], dev(lax.rem(z + 1, nz), x, y))

    def backward(q):
        return copy(bsend.at[q], suf.at[q], bs.at[q], br.at[q], dev(lax.rem(z + nz - 1, nz), x, y))

    def step(i):
        cf = i - LAG * z

        @pl.when((cf >= 0) & (cf < PAIRS))
        def _():
            @pl.when(z > 0)
            def _():
                forward(cf).wait_recv()

            @pl.when(z < nz - 1)
            def _():
                fsend[cf] = lanes_ref[cf, 0:1] * pre[cf] + fresh_ref[cf]
                forward(cf).start()

        cb = i - LAG * (nz - 1 - z)

        @pl.when((cb >= 0) & (cb < PAIRS))
        def _():
            @pl.when(z < nz - 1)
            def _():
                backward(cb).wait_recv()

            @pl.when(z > 0)
            def _():
                bsend[cb] = lanes_ref[cb, 0:1] * suf[cb] + entry_ref[cb]
                backward(cb).start()

    def chunk_of(ref, c):
        return ref[:, pl.ds(pl.multiple_of(c * LANES, LANES), LANES)]

    def masked(c):
        return chunk_of(gy_ref, c).astype(F32) * row_mask(len_ref)

    def alone(c):
        spread = spreader(c, NH)
        x_c = chunk_of(rx_ref, c)
        gf = masked(c)
        gy = gf.astype(BF16)
        xf = x_c.astype(F32)
        lane = iota((1, 128), 1) < HD
        q1 = []
        for pair in range(2):
            xp, gp = x_c[:, pair * 128 : pair * 128 + 128], gy[:, pair * 128 : pair * 128 + 128]
            total = [None] * 4
            for odd in range(2):
                j = 2 * pair + odd
                mine = jnp.logical_not(lane) if odd else lane
                xh = jnp.where(mine, xp, jnp.zeros_like(xp))
                gh = jnp.where(mine, gp, jnp.zeros_like(gp))
                col, dcol, arow = a_ch[c, :, j : j + 1], d_ch[c, :, j : j + 1], a_t[c, j : j + 1, :]
                found = [None, None]
                for b in range(4):
                    t0 = (b // 2) * 128
                    sl = slice(b * 64, b * 64 + 64)
                    g = gt[sl, t0:]
                    decay = jnp.exp(jnp.minimum(arow[:, t0:] - col[sl], 0.0))
                    hi, lo = split2(decay * g)
                    gpart = gh[t0:]
                    q = nn(hi, gpart) + nn(lo, gpart)
                    total[b] = q if total[b] is None else total[b] + q
                    k = decay * nt(xh[sl], gpart) * dcol[sl]
                    dgt[sl, t0:] += k
                    part = column(k * g)
                    at = b // 2
                    found[at] = part if found[at] is None else found[at] + part
                row[c, j : j + 1, :] = found[0]
                row[c, j : j + 1, 128:] += found[1]
            q1.append(jnp.concatenate(total, axis=0))
        q1 = jnp.concatenate(q1, axis=1)
        q1_ref[c] = q1
        acc1[...] += by_head(xf * q1, spread)
        outer[...] += by_head(fold8(xf * gf), spread)

    def with_grad(c):
        spread2 = spreader(c, 2 * NH)
        spread = spread2[:NH]
        xf = chunk_of(rx_ref, c).astype(F32)
        gf = masked(c)
        ghi, glo = split2(both(suf, c))
        rb_ = rb_ref[...]
        q2 = nn(rb_, ghi) + nn(rb_, glo)
        wide_w = nn(wcat[...], spread2)
        wide_skip = to_lanes(jnp.broadcast_to(skip_ref[...], (8, NH)), c)[0:1]
        found = factor * (nn(dcat[...], spread2) * q1_ref[c] + wide_w * q2 + wide_skip * gf)
        rdx_ref[:, pl.ds(pl.multiple_of(c * LANES, LANES), LANES)] = found.astype(BF16)
        acc2[...] += by_head(xf * q2, spread)
        whi, wlo = split2(wide_w * xf)
        rdb_ref[...] += nt(whi, ghi) + (nt(wlo, ghi) + nt(whi, glo))

    def with_state(c):
        spread2 = spreader(c, 2 * NH)
        spread = spread2[:NH]
        gf = masked(c)
        state = to_lanes(scan_ref[:, :NH], c)[0:1] * both(end, c) + both(pre, c)
        shi, slo = split2(state)
        rc_ = rc_ref[...]
        cs = nn(rc_, shi) + nn(rc_, slo)
        acc3[...] += by_head(gf * cs, spread)
        ehi, elo = split2(nn(ecat[...], spread2) * gf)
        rdc_ref[...] += nt(ehi, shi) + (nt(elo, shi) + nt(ehi, slo))
        inner[...] += by_head(fold8(state * both(suf, c)), spread)

    def prompt(c):
        spread2 = spreader(c, 2 * NH)
        spread = spread2[:NH]
        pxf = chunk_of(px_ref, c).astype(F32)
        pgrad = to_lanes(fol_ref[:, :NH], c)[1:2] * both(seed, c)
        ghi, glo = split2(pgrad)
        pb_ = pb_ref[...]
        q2 = nn(pb_, ghi) + nn(pb_, glo)
        wide_w = nn(pwcat[...], spread2)
        pdx_ref[:, pl.ds(pl.multiple_of(c * LANES, LANES), LANES)] = (wide_w * q2).astype(BF16)
        pacc[...] += by_head(pxf * q2, spread)
        whi, wlo = split2(wide_w * pxf)
        pdb_ref[...] += nt(whi, ghi) + (nt(wlo, ghi) + nt(whi, glo))
        eye = jnp.where(iota((NS, NS), 0) == iota((NS, NS), 1), 1.0, 0.0).astype(BF16)
        saved = nt(eye, ps_ref[pl.ds(pl.multiple_of(c * LANES, LANES), LANES), :])
        pinner[...] += by_head(fold8(saved * pgrad), spread)

    def closing():
        rate = -jnp.exp(alog)

        def close(zz, d, dstep, da, last):
            cum = exact_nn(upper(), da) + last
            ddt = (dstep + rate * cum) / (1.0 + jnp.exp(-zz))
            return ddt, cum * (rate * d)

        d, rr, e = d_in[...], r_in[...], e_in[...]
        dstep = acc1[...] + rr * acc2[...]
        erow = jnp.concatenate([row[k] for k in range(CHUNKS)], axis=0).T
        da = erow + e * acc3[...] - d * dstep
        last = e[TOK - 1 :] * column(inner[...]) + column(rr * d * acc2[...])
        ddt, dalog = close(z_in[...], d, dstep, da, last)
        ddt = factor * ddt
        rdd_ref[...] = ddt
        bias_sum, alog_sum = column(ddt), factor * column(dalog)
        skip_sum = factor * column(outer[...])

        d, rr = pd[...], pr[...]
        dstep = rr * pacc[...]
        weighted = d * dstep
        last = jnp.exp(column(rate * d)) * column(pinner[...]) + column(weighted)
        ddt, dalog = close(pz[...], d, dstep, -weighted, last)
        pdd_ref[...] = ddt
        terms[...] = jnp.zeros_like(terms)
        terms[0:1, :NH] = bias_sum + column(ddt)
        terms[1:2, :NH] = alog_sum + column(dalog)
        terms[2:3, :NH] = skip_sum

    def scores():
        keep = jnp.where(triangle(), dgt[...], 0.0)
        hi, lo = split2(keep)
        rdb_ref[...] = factor * (rdb_ref[...] + (nn(hi, rc_ref[...]) + nn(lo, rc_ref[...])))
        hi, lo = split2(keep.T)
        rdc_ref[...] = factor * (rdc_ref[...] + (nn(hi, rb_ref[...]) + nn(lo, rb_ref[...])))

    def terms_of(slots, at, send, recv, targets):
        mine = slots.at[at]
        return [copy(mine, mine, send.at[i], recv.at[i], to) for i, to in enumerate(targets)]

    def gather(slots, at, size, send, recv, targets):
        slots[at] = terms[...]
        copies = terms_of(slots, at, send, recv, targets)
        start(copies)
        wait_recv(copies)
        total = slots[0]
        for i in range(1, size):
            total = total + slots[i]
        terms[...] = total
        return copies

    start(tiles_z())
    start(tiles_y())
    prepare()
    first_full = -(-LAG * (nz - 1) // 2)
    turns = first_full + CHUNKS

    def turn(j, carry):
        step(2 * j)

        @pl.when(j < CHUNKS)
        def _():
            alone(j)

        step(2 * j + 1)

        @pl.when(j >= first_full)
        def _():
            with_grad(j - first_full)

        return carry

    done = 0
    for mark, act in zip(MARKS, (do1, do2, do3, do4, do5, do6)):
        lax.fori_loop(done, mark, turn, 0)
        act()
        done = mark
    lax.fori_loop(done, turns, turn, 0)
    do7()

    def rest(c, carry):
        with_state(c)
        prompt(c)
        return carry

    lax.fori_loop(0, CHUNKS, rest, 0)
    closing()
    pending = gather(sx, x, nx, xs_s, xs_r, [dev(z, t, y) for t in xs])
    scores()
    pending += gather(sy, y, ny, ys_s, ys_r, [dev(z, x, t) for t in ys])
    pending += gather(sz, z, nz, zs_s, zs_r, [dev(t, x, y) for t in zs])
    if ndp > 1:
        pending += gather(sd, dp, ndp, ds_s, ds_r, ds)
    small_ref[...] = terms[...]
    wait_send(pending)
    drain()


def factors(count):
    first = 1
    while first * first < count:
        first *= 2
    return first, count // first


def main_call(mesh_shape, *args):
    nz = mesh_shape["ctx"]
    nx, ny = factors(mesh_shape["resp"])
    half = PAIRS // 2
    pa, pb = half // nx, half // ny
    qa, qb = pa // ny, pb // nx
    rows = NS // nz
    vmem = pl.BlockSpec(memory_space=pltpu.VMEM)
    smem = pl.BlockSpec(memory_space=pltpu.SMEM)
    v = lambda *shape: pltpu.VMEM(shape, F32)
    b = lambda *shape: pltpu.VMEM(shape, BF16)
    buf = lambda *lead: pltpu.VMEM(lead + (128,), F32)
    sem = lambda n: pltpu.SemaphoreType.DMA((n,))
    out = jax.ShapeDtypeStruct
    return pl.pallas_call(
        functools.partial(main_kernel, nz, nx, ny),
        out_shape=(
            out((TOK, NH * HD), BF16),
            out((TOK, NS), F32),
            out((TOK, NH), F32),
            out((TOK, NH * HD), BF16),
            out((TOK, NS), F32),
            out((TOK, NS), F32),
            out((TOK, NH), F32),
            out((8, 128), F32),
        ),
        in_specs=[smem] * 2 + [vmem] * 16,
        out_specs=(vmem,) * 8,
        scratch_shapes=[
            v(CHUNKS, TOK, PER), v(CHUNKS, TOK, PER), v(CHUNKS, PER, TOK), v(TOK, TOK), v(TOK, TOK),
            v(CHUNKS, TOK, LANES), b(TOK, 2 * NH), b(TOK, 2 * NH), b(TOK, 2 * NH),
            v(TOK, NH), v(TOK, NH), v(TOK, NH), v(TOK, NH), v(CHUNKS, PER, TOK),
            v(TOK, NH), v(TOK, NH), v(TOK, NH), v(8, NH), v(8, NH),
            b(TOK, 2 * NH), v(TOK, NH), v(TOK, NH), v(TOK, NH), v(TOK, NH), v(8, NH), buf(8), buf(8), buf(PAIRS, 8),
        ]
        + [buf(PAIRS, NS)] * 7
        + [
            buf(nx - 1, pa, NS), buf(ny - 1, pb, NS), buf(pa, NS), buf(pb, NS), buf(ny - 1, qa, NS),
            buf(nx - 1, qb, NS), buf(qa + qb, NS), buf(nz - 1, qa + qb, rows), buf(2 * (qa + qb), NS),
            buf(pa, NS), buf(pb, NS), buf(qa + qb, NS),
            buf(nz, 8), buf(ny, 8), buf(nx, 8), buf(nz, 8), buf(8), buf(8),
            buf(nx, 8), buf(ny, 8), buf(nz, 8), buf(2, 8), buf(8),
        ]
        + [sem(PAIRS)] * 4
        + [sem(nx + ny)] * 4
        + [sem(nz)] * 4
        + [sem(2 * (nx + ny))] * 4
        + [sem(nx + ny), sem(2), sem(nx + ny), sem(2), sem(nz), sem(1)]
        + [sem(nz)] * 2 + [sem(ny)] * 2 + [sem(nx)] * 2 + [sem(nz)] * 2
        + [sem(nx)] * 2 + [sem(ny)] * 2 + [sem(nz)] * 2 + [sem(2)] * 2,
        compiler_params=pltpu.CompilerParams(collective_id=0, has_side_effects=True, vmem_limit_bytes=LIMIT),
        name="main",
    )(*args)


def body(
    mesh_shape,
    prompt_x, prompt_b, prompt_dt, prompt_states, resp_x, resp_b, resp_c, resp_dt, grad_out, lengths, advantages,
    dt_bias, a_log, skip,
):
    nz = mesh_shape["ctx"]
    px, pb, pdt = prompt_x[0], prompt_b[0], prompt_dt[0]
    ps = prompt_states.reshape(NH * HD, NS)
    rx, rb, rc, rdt, gy = resp_x[0, 0], resp_b[0, 0], resp_c[0, 0], resp_dt[0, 0], grad_out[0, 0]
    bias, alog = dt_bias[None], a_log[None]
    factor = advantages * float(nz * TOK) / lengths.astype(F32)
    fresh, entry, end, tile = first_call(lengths, rx, rb, rc, rdt, gy, px, pb, pdt, ps, bias, alog)
    pdx, pdb, pdd, rdx, rdb, rdc, rdd, small = main_call(
        mesh_shape, lengths, factor, fresh, entry, end, tile,
        rx, rb, rc, rdt, gy, px, pb, pdt, ps, bias, alog, skip[None],
    )
    return (
        pdx[None], pdb[None], pdd[None], rdx[None, None], rdb[None, None], rdc[None, None], rdd[None, None],
        small[0, :NH], small[1, :NH], small[2, :NH],
    )


def solution(mesh):
    wide = P("dp", ("ctx", "resp"), None)
    long = P("dp", "resp", "ctx", None)
    in_specs = (
        wide, wide, wide, P("dp", ("ctx", "resp"), None, None, None), long, long, long, long, long,
        P("dp", "resp"), P("dp", "resp"), P(), P(), P(),
    )
    out_specs = (wide, wide, wide, long, long, long, long, P(), P(), P())
    return jax.shard_map(
        functools.partial(body, dict(mesh.shape)), mesh=mesh, in_specs=in_specs, out_specs=out_specs, check_vma=False
    )
```

```python
import functools

import jax
import jax.numpy as jnp
from jax import lax
from jax.experimental import pallas as pl
from jax.experimental.pallas import tpu as pltpu
from jax.sharding import PartitionSpec as P

MESH = pl.DeviceIdType.MESH
F32 = jnp.float32
BF16 = jnp.bfloat16
TOK = 256
LANES = 256
PER = 4
NH = 64
HD = 64
NS = 128
CHUNKS = 16
PAIRS = 32
LIMIT = 56 * 1024 * 1024


def nn(a, b):
    return lax.dot_general(a, b, (((1,), (0,)), ((), ())), preferred_element_type=F32)


def nt(a, b):
    return lax.dot_general(a, b, (((1,), (1,)), ((), ())), preferred_element_type=F32)


def split2(v):
    hi = v.astype(BF16)
    return hi, (v - hi.astype(F32)).astype(BF16)


def split3(v):
    hi = v.astype(BF16)
    rest = v - hi.astype(F32)
    mid = rest.astype(BF16)
    return hi, mid, (rest - mid.astype(F32)).astype(BF16)


def exact_nn(tri, v):
    hi, mid, lo = split3(v)
    return nn(tri, hi) + (nn(tri, mid) + nn(tri, lo))


def iota(shape, dim):
    return lax.broadcasted_iota(jnp.int32, shape, dim)


def lower():
    return jnp.where(iota((TOK, TOK), 0) >= iota((TOK, TOK), 1), 1.0, 0.0).astype(BF16)


def upper():
    return jnp.where(iota((TOK, TOK), 0) <= iota((TOK, TOK), 1), 1.0, 0.0).astype(BF16)


def spreader(c, rows):
    head = iota((rows, LANES), 0) & (NH - 1)
    lane = iota((rows, LANES), 1) >> 6
    return jnp.where(head == lane + c * PER, 1.0, 0.0).astype(BF16)


def steps(dt, bias, alog):
    z = dt + bias
    d = jnp.maximum(z, 0.0) + jnp.log1p(jnp.exp(-jnp.abs(z)))
    rate = -jnp.exp(alog)
    a = exact_nn(lower(), rate * d)
    return z, d, rate, a


def cat2(v):
    hi, lo = split2(v)
    return jnp.concatenate([hi, lo], axis=1)


def by_head(v, spread):
    hi, lo = split2(v)
    return nt(hi, spread) + nt(lo, spread)


def fold8(v):
    total = v[0:8]
    for at in range(8, v.shape[0], 8):
        total = total + v[at : at + 8]
    return total


def cat3(v):
    return jnp.concatenate(split3(v), axis=1)


def column(v):
    return jnp.sum(v, axis=0, keepdims=True)


def triangle():
    return iota((TOK, TOK), 0) <= iota((TOK, TOK), 1)


def both(ref, c):
    return jnp.concatenate([ref[2 * c], ref[2 * c + 1]], axis=1)


def row_mask(length_ref):
    position = lax.axis_index("ctx") * TOK + iota((TOK, 1), 0)
    return jnp.where(position < length_ref[0, 0], 1.0, 0.0)


LAG = 3
MARKS = (5, 7, 8, 9, 10, 11, 12, 13)


def main_kernel(
    nz, nx, ny,
    len_ref, fac_ref,
    rx_ref, rb_ref, rc_ref, rdt_ref, gy_ref, px_ref, pb_ref, pdt_ref, ps_ref, bias_ref, alog_ref, skip_ref,
    pdx_ref, pdb_ref, pdd_ref, rdx_ref, rdb_ref, rdc_ref, rdd_ref, small_ref,
    a_ch, d_ch, a_t, gt, dgt, q1_ref, dcat, wcat, ecat, e_in, r_in, d_in, z_in, row, acc1, acc2, acc3, inner, outer,
    pwcat, pr, pd, pz, pacc, pinner, scan_ref, fol_ref, lanes_ref,
    bt, ct, pbt, pecat, tile_ref, fresh_ref, entry_ref, end_in,
    pre, suf, fsend, bsend, seedc, seed, end, ra, rb, sa, sb, ra2, rb2, own, rz, zfull, enda, endb, endown,
    tz, ty, tx, tp, mine_y, mine_x, sx, sy, sz, sd, terms,
    fs, fr, bs, br, s1, r1, s2, r2, s3, r3, s4, r4, s5, r5, s6, r6, e1s, e1r, e2s, e2r, e3s, e3r,
    tzs, tzr, tys, tyr, txs, txr, tps, tpr, xs_s, xs_r, ys_s, ys_r, zs_s, zs_r, ds_s, ds_r,
):
    dp, z, r = lax.axis_index("dp"), lax.axis_index("ctx"), lax.axis_index("resp")
    ndp = lax.axis_size("dp")
    x, y = r // ny, lax.rem(r, ny)
    half = PAIRS // 2
    pa, pb = half // nx, half // ny
    qa, qb = pa // ny, pb // nx
    rows = NS // nz
    dev = lambda zz, xx, yy: (dp, zz, xx * ny + yy)
    xs = [lax.rem(x + i, nx) for i in range(1, nx)]
    ys = [lax.rem(y + i, ny) for i in range(1, ny)]
    zs = [lax.rem(z + i, nz) for i in range(1, nz)]
    ds = [(lax.rem(dp + i, ndp), z, r) for i in range(1, ndp)]
    factor = fac_ref[0, 0]

    barrier = pltpu.get_barrier_semaphore()
    partners = [dev(z, t, y) for t in xs] + [dev(z, x, t) for t in ys] + [dev(t, x, y) for t in zs] + ds
    for partner in partners:
        pl.semaphore_signal(barrier, inc=1, device_id=partner, device_id_type=MESH)

    bias, alog = bias_ref[...], alog_ref[...]

    def prepare():
        zz, d, _, a = steps(rdt_ref[...].T, bias, alog)
        z_in[...] = zz
        d_in[...] = d
        at = a.T
        for k in range(CHUNKS):
            a_ch[k] = a[:, k * PER : k * PER + PER]
            d_ch[k] = d[:, k * PER : k * PER + PER]
            a_t[k] = at[k * PER : k * PER + PER]
        e = jnp.exp(a)
        rr = jnp.exp(a[TOK - 1 :, :] - a)
        e_in[...] = e
        r_in[...] = rr
        dcat[...] = cat2(d)
        wcat[...] = cat2(rr * d)
        ecat[...] = cat2(e)
        tile_ref[...] = jnp.ones_like(tile_ref)
        tile_ref[0:1, :NH] = e[TOK - 1 :]
        zz, d, _, a = steps(pdt_ref[...].T, bias, alog)
        pz[...] = zz
        pd[...] = d
        rr = jnp.exp(a[TOK - 1 :, :] - a)
        pr[...] = rr
        pwcat[...] = cat2(rr * d)
        tile_ref[1:2, :NH] = jnp.exp(a[TOK - 1 :, :])
        bt[...] = rb_ref[...].astype(F32).T.astype(BF16)
        ct[...] = rc_ref[...].astype(F32).T.astype(BF16)

    def prepare_rest():
        scores = nt(rb_ref[...], rc_ref[...])
        gt[...] = jnp.where(triangle(), scores, 0.0)
        dgt[...] = jnp.zeros_like(dgt)
        for acc in (acc1, acc2, acc3, inner, outer, pacc, pinner, rdb_ref, rdc_ref, pdb_ref):
            acc[...] = jnp.zeros_like(acc)
        for c in range(CHUNKS):
            put(lanes_ref, c, to_lanes(tile_ref[:, :NH], c))

        @pl.when(z == 0)
        def _():
            pre[...] = jnp.zeros_like(pre)

        @pl.when(z == nz - 1)
        def _():
            suf[...] = jnp.zeros_like(suf)

    def to_lanes(v, c):
        return nn(cat3(v), spreader(c, 3 * NH))

    def put(ref, c, value):
        ref[2 * c] = value[:, :128]
        ref[2 * c + 1] = value[:, 128:]

    def chunk_of(ref, c):
        return ref[:, pl.ds(pl.multiple_of(c * LANES, LANES), LANES)]

    def masked(c):
        return chunk_of(gy_ref, c).astype(F32) * row_mask(len_ref)

    def add_entry(c):
        hi, lo = split2(nn(ecat[...], spreader(c, 2 * NH)) * masked(c))
        put(entry_ref, c, nn(ct[...], hi) + nn(ct[...], lo))

    def add_fresh(c):
        hi, lo = split2(nn(wcat[...], spreader(c, 2 * NH)) * chunk_of(rx_ref, c).astype(F32))
        put(fresh_ref, c, nn(bt[...], hi) + nn(bt[...], lo))

    def saved_state(c):
        eye = jnp.where(iota((NS, NS), 0) == iota((NS, NS), 1), 1.0, 0.0).astype(BF16)
        return nt(eye, ps_ref[pl.ds(pl.multiple_of(c * LANES, LANES), LANES), :])

    def last_state():
        pbt[...] = pb_ref[...].astype(F32).T.astype(BF16)
        pecat[...] = cat2(jnp.broadcast_to(tile_ref[1:2, :NH], (NS, NH)))

        def one(c, carry):
            spread = spreader(c, 2 * NH)
            hi, lo = split2(nn(pwcat[...], spread) * chunk_of(px_ref, c).astype(F32))
            put(end_in, c, nn(pecat[...], spread) * saved_state(c) + (nn(pbt[...], hi) + nn(pbt[...], lo)))
            return carry

        lax.fori_loop(0, CHUNKS, one, 0, unroll=2)

    prepare()
    pl.semaphore_wait(barrier, len(partners))

    def copy(src, dst, send, recv, to):
        return pltpu.make_async_remote_copy(
            src_ref=src, dst_ref=dst, send_sem=send, recv_sem=recv, device_id=to, device_id_type=MESH
        )

    def start(copies):
        for one in copies:
            one.start()

    def wait_send(copies):
        for one in copies:
            one.wait_send()

    def wait_recv(copies):
        for one in copies:
            one.wait_recv()

    def tiles_z():
        return [copy(tile_ref, tz.at[i], tzs.at[i], tzr.at[i], dev(t, x, y)) for i, t in enumerate(zs)]

    def tiles_y():
        return [copy(tile_ref, ty.at[i], tys.at[i], tyr.at[i], dev(z, x, t)) for i, t in enumerate(ys)]

    def tiles_x():
        return [copy(mine_y, tx.at[i], txs.at[i], txr.at[i], dev(z, t, y)) for i, t in enumerate(xs)]

    def tiles_p():
        return [copy(mine_x, tp.at[i], tps.at[i], tpr.at[i], dev(t, x, y)) for i, t in enumerate(zs)]

    def before(slots, at, size):
        total = jnp.ones((8, 128), F32)
        for i in range(size - 1):
            total = total * jnp.where(i + 1 <= at, slots[i], 1.0)
        return total

    def after(slots, at, size):
        total = jnp.ones((8, 128), F32)
        for i in range(size - 1):
            total = total * jnp.where(i + 1 > at, slots[i], 1.0)
        return total

    def phase1():
        return [
            copy(seedc.at[pl.ds(t * pa, pa)], ra.at[i], s1.at[i], r1.at[i], dev(z, t, y))
            for i, t in enumerate(xs)
        ] + [
            copy(seedc.at[pl.ds(half + t * pb, pb)], rb.at[i], s1.at[nx + i], r1.at[nx + i], dev(z, x, t))
            for i, t in enumerate(ys)
        ]

    def phase2():
        return [
            copy(sa.at[pl.ds(t * qa, qa)], ra2.at[i], s2.at[i], r2.at[i], dev(z, x, t))
            for i, t in enumerate(ys)
        ] + [
            copy(sb.at[pl.ds(t * qb, qb)], rb2.at[i], s2.at[ny + i], r2.at[ny + i], dev(z, t, y))
            for i, t in enumerate(xs)
        ]

    def phase3():
        return [
            copy(own.at[:, pl.ds(t * rows, rows)], rz.at[i], s3.at[i], r3.at[i], dev(t, x, y))
            for i, t in enumerate(zs)
        ]

    def phase4(k):
        mine = zfull.at[pl.ds(k * (qa + qb), qa + qb), pl.ds(z * rows, rows)]
        return [copy(mine, mine, s4.at[k * nz + i], r4.at[k * nz + i], dev(t, x, y)) for i, t in enumerate(zs)]

    la, lb = x * pa + y * qa, half + y * pb + x * qb

    def phase5(k):
        whole, found = (seed, end)[k], []
        for i, t in enumerate(ys):
            at, src = k * (nx + ny) + i, zfull.at[pl.ds(k * (qa + qb), qa)]
            found.append(copy(src, whole.at[pl.ds(la, qa)], s5.at[at], r5.at[at], dev(z, x, t)))
        for i, t in enumerate(xs):
            at, src = k * (nx + ny) + ny + i, zfull.at[pl.ds(k * (qa + qb) + qa, qb)]
            found.append(copy(src, whole.at[pl.ds(lb, qb)], s5.at[at], r5.at[at], dev(z, t, y)))
        return found

    def phase6(k):
        whole, found = (seed, end)[k], []
        for i, t in enumerate(xs):
            at, mine = k * (nx + ny) + i, whole.at[pl.ds(x * pa, pa)]
            found.append(copy(mine, mine, s6.at[at], r6.at[at], dev(z, t, y)))
        for i, t in enumerate(ys):
            at, mine = k * (nx + ny) + nx + i, whole.at[pl.ds(half + y * pb, pb)]
            found.append(copy(mine, mine, s6.at[at], r6.at[at], dev(z, x, t)))
        return found

    on_plane = z == nz - 1
    on_x, on_y = on_plane & (x == nx - 1), on_plane & (y == ny - 1)
    source = on_x & on_y

    def end1a(i, t):
        return copy(end_in.at[pl.ds(t * pa, pa)], enda, e1s.at[i], e1r.at[0], dev(z, t, y))

    def end1b(i, t):
        return copy(end_in.at[pl.ds(half + t * pb, pb)], endb, e1s.at[nx + i], e1r.at[1], dev(z, x, t))

    def end1():
        return [end1a(i, t) for i, t in enumerate(xs)] + [end1b(i, t) for i, t in enumerate(ys)]

    def end2a(i, t):
        return copy(enda.at[pl.ds(t * qa, qa)], endown.at[pl.ds(0, qa)], e2s.at[i], e2r.at[0], dev(z, x, t))

    def end2b(i, t):
        return copy(endb.at[pl.ds(t * qb, qb)], endown.at[pl.ds(qa, qb)], e2s.at[ny + i], e2r.at[1], dev(z, t, y))

    def end3(i, t):
        at = pl.ds(t * rows, rows)
        return copy(
            endown.at[:, at], zfull.at[pl.ds(qa + qb, qa + qb), at], e3s.at[i], e3r.at[0], dev(t, x, y)
        )

    def each(make, targets):
        return [make(i, t) for i, t in enumerate(targets)]

    def do1():
        wait_recv(tiles_z())
        scan = before(tz, z, nz)
        scan_ref[...] = scan
        for c in range(CHUNKS):
            wide = to_lanes(scan[:, :NH] * factor, c)
            seedc[2 * c] = entry_ref[2 * c] * wide[0:1, :128]
            seedc[2 * c + 1] = entry_ref[2 * c + 1] * wide[0:1, 128:]
        start(phase1())
        wait_recv(tiles_y())
        fol_ref[...] = after(ty, y, ny)
        total = tile_ref[...]
        for i in range(ny - 1):
            total = total * ty[i]
        mine_y[...] = total
        start(tiles_x())

        @pl.when(source)
        def _():
            last_state()
            start(end1())

    def do2():
        wait_recv(phase1())
        for q in range(pa):
            total = seedc[x * pa + q]
            for i in range(nx - 1):
                total = total + ra[i, q]
            sa[q] = total
        for q in range(pb):
            total = seedc[half + y * pb + q]
            for i in range(ny - 1):
                total = total + rb[i, q]
            sb[q] = total
        start(phase2())
        wait_recv(tiles_x())
        fol_ref[...] = fol_ref[...] * after(tx, x, nx)
        total = mine_y[...]
        for i in range(nx - 1):
            total = total * tx[i]
        mine_x[...] = total
        start(tiles_p())

    def end_2():
        @pl.when(source)
        def _():
            enda[...] = end_in[pl.ds(x * pa, pa)]
            endb[...] = end_in[pl.ds(half + y * pb, pb)]

        @pl.when(on_y)
        def _():
            @pl.when(x != nx - 1)
            def _():
                end1a(0, xs[0]).wait_recv()

            start(each(end2a, ys))
            for q in range(qa):
                endown[q] = enda[y * qa + q]

        @pl.when(on_x)
        def _():
            @pl.when(y != ny - 1)
            def _():
                end1b(0, ys[0]).wait_recv()

            start(each(end2b, xs))
            for q in range(qb):
                endown[qa + q] = endb[x * qb + q]

    def do3():
        wait_recv(phase2())
        wait_send(phase1())
        for q in range(qa):
            total = sa[y * qa + q]
            for i in range(ny - 1):
                total = total + ra2[i, q]
            own[q] = total
        for q in range(qb):
            total = sb[x * qb + q]
            for i in range(nx - 1):
                total = total + rb2[i, q]
            own[qa + q] = total
        start(phase3())

    def end_3():
        @pl.when(on_plane)
        def _():
            @pl.when(y != ny - 1)
            def _():
                end2a(0, ys[0]).wait_recv()

            @pl.when(x != nx - 1)
            def _():
                end2b(0, xs[0]).wait_recv()

            start(each(end3, zs))
            mine = pl.ds(z * rows, rows)
            for q in range(qa + qb):
                zfull[qa + qb + q, mine] = endown[q, mine]

    def do4():
        wait_recv(phase3())
        mine = pl.ds(z * rows, rows)
        for q in range(qa + qb):
            total = own[q, mine]
            for i in range(nz - 1):
                total = total + rz[i, q]
            zfull[q, mine] = total
        start(phase4(0))
        wait_recv(tiles_p())
        fol_ref[...] = fol_ref[...] * after(tp, z, nz)

    def end_4():
        @pl.when(jnp.logical_not(on_plane))
        def _():
            end3(0, zs[0]).wait_recv()

        start(phase4(1))

    def spread_5(k):
        whole = (seed, end)[k]
        wait_recv(phase4(k))
        start(phase5(k))
        for q in range(qa):
            whole[la + q] = zfull[k * (qa + qb) + q]
        for q in range(qb):
            whole[lb + q] = zfull[k * (qa + qb) + qa + q]

    def spread_6(k):
        wait_recv(phase5(k))
        start(phase6(k))

    def drain():
        for phase in (phase2, phase3, tiles_z, tiles_y, tiles_x, tiles_p):
            wait_send(phase())
        for phase in (phase4, phase5, phase6):
            wait_send(phase(0))
            wait_send(phase(1))

        @pl.when(source)
        def _():
            wait_send(end1())

        @pl.when(on_y)
        def _():
            wait_send(each(end2a, ys))

        @pl.when(on_x)
        def _():
            wait_send(each(end2b, xs))

        @pl.when(on_plane)
        def _():
            wait_send(each(end3, zs))

        def finish(q, carry):
            @pl.when(z < nz - 1)
            def _():
                forward(q).wait_send()

            @pl.when(z > 0)
            def _():
                backward(q).wait_send()

            return carry

        lax.fori_loop(0, PAIRS, finish, 0)

    def forward(q):
        return copy(fsend.at[q], pre.at[q], fs.at[q], fr.at[q], dev(lax.rem(z + 1, nz), x, y))

    def backward(q):
        return copy(bsend.at[q], suf.at[q], bs.at[q], br.at[q], dev(lax.rem(z + nz - 1, nz), x, y))

    def step(i):
        cf = i - LAG * z

        @pl.when((cf >= 0) & (cf < PAIRS))
        def _():
            @pl.when(z > 0)
            def _():
                forward(cf).wait_recv()

            @pl.when(z < nz - 1)
            def _():
                fsend[cf] = lanes_ref[cf, 0:1] * pre[cf] + fresh_ref[cf]
                forward(cf).start()

        cb = i - LAG * (nz - 1 - z)

        @pl.when((cb >= 0) & (cb < PAIRS))
        def _():
            @pl.when(z < nz - 1)
            def _():
                backward(cb).wait_recv()

            @pl.when(z > 0)
            def _():
                bsend[cb] = lanes_ref[cb, 0:1] * suf[cb] + entry_ref[cb]
                backward(cb).start()

    def alone(c):
        spread = spreader(c, NH)
        x_c = chunk_of(rx_ref, c)
        gf = masked(c)
        gy = gf.astype(BF16)
        xf = x_c.astype(F32)
        lane = iota((1, 128), 1) < HD
        q1 = []
        for pair in range(2):
            xp, gp = x_c[:, pair * 128 : pair * 128 + 128], gy[:, pair * 128 : pair * 128 + 128]
            total = [None] * 4
            for odd in range(2):
                j = 2 * pair + odd
                mine = jnp.logical_not(lane) if odd else lane
                xh = jnp.where(mine, xp, jnp.zeros_like(xp))
                gh = jnp.where(mine, gp, jnp.zeros_like(gp))
                col, dcol, arow = a_ch[c, :, j : j + 1], d_ch[c, :, j : j + 1], a_t[c, j : j + 1, :]
                found = [None, None]
                for b in range(4):
                    t0 = (b // 2) * 128
                    sl = slice(b * 64, b * 64 + 64)
                    g = gt[sl, t0:]
                    decay = jnp.exp(jnp.minimum(arow[:, t0:] - col[sl], 0.0))
                    hi, lo = split2(decay * g)
                    gpart = gh[t0:]
                    q = nn(hi, gpart) + nn(lo, gpart)
                    total[b] = q if total[b] is None else total[b] + q
                    k = decay * nt(xh[sl], gpart) * dcol[sl]
                    dgt[sl, t0:] += k
                    part = column(k * g)
                    at = b // 2
                    found[at] = part if found[at] is None else found[at] + part
                row[c, j : j + 1, :] = found[0]
                row[c, j : j + 1, 128:] += found[1]
            q1.append(jnp.concatenate(total, axis=0))
        q1 = jnp.concatenate(q1, axis=1)
        q1_ref[c] = q1
        acc1[...] += by_head(xf * q1, spread)
        outer[...] += by_head(fold8(xf * gf), spread)

    def with_grad(c):
        spread2 = spreader(c, 2 * NH)
        spread = spread2[:NH]
        xf = chunk_of(rx_ref, c).astype(F32)
        gf = masked(c)
        ghi, glo = split2(both(suf, c))
        rb_ = rb_ref[...]
        q2 = nn(rb_, ghi) + nn(rb_, glo)
        wide_w = nn(wcat[...], spread2)
        wide_skip = to_lanes(jnp.broadcast_to(skip_ref[...], (8, NH)), c)[0:1]
        found = factor * (nn(dcat[...], spread2) * q1_ref[c] + wide_w * q2 + wide_skip * gf)
        rdx_ref[:, pl.ds(pl.multiple_of(c * LANES, LANES), LANES)] = found.astype(BF16)
        acc2[...] += by_head(xf * q2, spread)
        whi, wlo = split2(wide_w * xf)
        rdb_ref[...] += nt(whi, ghi) + (nt(wlo, ghi) + nt(whi, glo))

    def with_state(c):
        spread2 = spreader(c, 2 * NH)
        spread = spread2[:NH]
        gf = masked(c)
        state = to_lanes(scan_ref[:, :NH], c)[0:1] * both(end, c) + both(pre, c)
        shi, slo = split2(state)
        rc_ = rc_ref[...]
        cs = nn(rc_, shi) + nn(rc_, slo)
        acc3[...] += by_head(gf * cs, spread)
        ehi, elo = split2(nn(ecat[...], spread2) * gf)
        rdc_ref[...] += nt(ehi, shi) + (nt(elo, shi) + nt(ehi, slo))
        inner[...] += by_head(fold8(state * both(suf, c)), spread)

    def prompt(c):
        spread = spreader(c, NH)
        pxf = chunk_of(px_ref, c).astype(F32)
        pgrad = to_lanes(fol_ref[:, :NH], c)[1:2] * both(seed, c)
        put(seedc, c, pgrad)
        ghi, glo = split2(pgrad)
        pb_ = pb_ref[...]
        q2 = nn(pb_, ghi) + nn(pb_, glo)
        q1_ref[c] = q2
        pacc[...] += by_head(pxf * q2, spread)
        pinner[...] += by_head(fold8(saved_state(c) * pgrad), spread)

    def prompt_rest(c):
        pxf = chunk_of(px_ref, c).astype(F32)
        ghi, glo = split2(both(seedc, c))
        wide_w = nn(pwcat[...], spreader(c, 2 * NH))
        pdx_ref[:, pl.ds(pl.multiple_of(c * LANES, LANES), LANES)] = (wide_w * q1_ref[c]).astype(BF16)
        whi, wlo = split2(wide_w * pxf)
        pdb_ref[...] += nt(whi, ghi) + (nt(wlo, ghi) + nt(whi, glo))

    rate = -jnp.exp(alog)

    def close(zz, d, dstep, da, last):
        cum = exact_nn(upper(), da) + last
        ddt = (dstep + rate * cum) / (1.0 + jnp.exp(-zz))
        return ddt, cum * (rate * d)

    def close_resp():
        d, rr, e = d_in[...], r_in[...], e_in[...]
        dstep = acc1[...] + rr * acc2[...]
        erow = jnp.concatenate([row[k] for k in range(CHUNKS)], axis=0).T
        da = erow + e * acc3[...] - d * dstep
        last = e[TOK - 1 :] * column(inner[...]) + column(rr * d * acc2[...])
        ddt, dalog = close(z_in[...], d, dstep, da, last)
        ddt = factor * ddt
        rdd_ref[...] = ddt.T
        terms[...] = jnp.zeros_like(terms)
        terms[0:1, :NH] = column(ddt)
        terms[1:2, :NH] = factor * column(dalog)
        terms[2:3, :NH] = factor * column(outer[...])

    def close_prompt():
        d, rr = pd[...], pr[...]
        dstep = rr * pacc[...]
        weighted = d * dstep
        last = jnp.exp(column(rate * d)) * column(pinner[...]) + column(weighted)
        ddt, dalog = close(pz[...], d, dstep, -weighted, last)
        pdd_ref[...] = ddt.T
        terms[0:1, :NH] += column(ddt)
        terms[1:2, :NH] += column(dalog)

    def scores():
        keep = jnp.where(triangle(), dgt[...], 0.0)
        hi, lo = split2(keep)
        rdb_ref[...] = factor * (rdb_ref[...] + (nn(hi, rc_ref[...]) + nn(lo, rc_ref[...])))
        hi, lo = split2(keep.T)
        rdc_ref[...] = factor * (rdc_ref[...] + (nn(hi, rb_ref[...]) + nn(lo, rb_ref[...])))

    def terms_of(slots, at, send, recv, targets):
        mine = slots.at[at]
        return [copy(mine, mine, send.at[i], recv.at[i], to) for i, to in enumerate(targets)]

    def gather(slots, at, size, send, recv, targets, beside):
        slots[at] = terms[...]
        copies = terms_of(slots, at, send, recv, targets)
        start(copies)
        beside()
        wait_recv(copies)
        total = slots[0]
        for i in range(1, size):
            total = total + slots[i]
        terms[...] = total
        return copies

    start(tiles_z())
    start(tiles_y())

    def looped(work, lo, hi, unroll=2):
        def one(c, carry):
            work(c)
            return carry

        lax.fori_loop(lo, hi, one, 0, unroll=unroll)

    looped(add_entry, 0, CHUNKS)
    do1()
    prepare_rest()
    first_full = -(-LAG * (nz - 1) // 2)
    turns = first_full + CHUNKS

    def turn(j, carry):
        @pl.when(j < CHUNKS)
        def _():
            add_fresh(j)

        step(2 * j)

        @pl.when(j < CHUNKS)
        def _():
            alone(j)

        step(2 * j + 1)

        @pl.when(j >= first_full)
        def _():
            with_grad(j - first_full)

        return carry

    done = 0
    acts = (
        lambda: (do2(), end_2()), lambda: (do3(), end_3()), end_4, do4,
        lambda: spread_5(1), lambda: spread_5(0), lambda: spread_6(1), lambda: spread_6(0),
    )
    for mark, act in zip(MARKS, acts):
        lax.fori_loop(done, mark, turn, 0)
        act()
        done = mark
    lax.fori_loop(done, turns, turn, 0)
    wait_recv(phase6(1))
    looped(with_state, 0, CHUNKS)
    close_resp()
    wait_recv(phase6(0))
    looped(prompt, 0, CHUNKS)
    close_prompt()
    part = CHUNKS // 4
    pending = gather(sx, x, nx, xs_s, xs_r, [dev(z, t, y) for t in xs], lambda: looped(prompt_rest, 0, part))
    pending += gather(
        sy, y, ny, ys_s, ys_r, [dev(z, x, t) for t in ys], lambda: looped(prompt_rest, part, 2 * part)
    )
    pending += gather(
        sz, z, nz, zs_s, zs_r, [dev(t, x, y) for t in zs], lambda: looped(prompt_rest, 2 * part, CHUNKS)
    )
    pending += gather(sd, dp, ndp, ds_s, ds_r, ds, scores)
    small_ref[...] = terms[...]
    wait_send(pending)
    drain()


def factors(count):
    first = 1
    while first * first < count:
        first *= 2
    return first, count // first


def main_call(mesh_shape, *args):
    nz = mesh_shape["ctx"]
    nx, ny = factors(mesh_shape["resp"])
    half = PAIRS // 2
    pa, pb = half // nx, half // ny
    qa, qb = pa // ny, pb // nx
    rows = NS // nz
    vmem = pl.BlockSpec(memory_space=pltpu.VMEM)
    smem = pl.BlockSpec(memory_space=pltpu.SMEM)
    v = lambda *shape: pltpu.VMEM(shape, F32)
    b = lambda *shape: pltpu.VMEM(shape, BF16)
    buf = lambda *lead: pltpu.VMEM(lead + (128,), F32)
    sem = lambda n: pltpu.SemaphoreType.DMA((n,))
    out = jax.ShapeDtypeStruct
    return pl.pallas_call(
        functools.partial(main_kernel, nz, nx, ny),
        out_shape=(
            out((TOK, NH * HD), BF16),
            out((TOK, NS), F32),
            out((NH, TOK), F32),
            out((TOK, NH * HD), BF16),
            out((TOK, NS), F32),
            out((TOK, NS), F32),
            out((NH, TOK), F32),
            out((8, 128), F32),
        ),
        in_specs=[smem] * 2 + [vmem] * 12,
        out_specs=(vmem,) * 8,
        scratch_shapes=[
            v(CHUNKS, TOK, PER), v(CHUNKS, TOK, PER), v(CHUNKS, PER, TOK), v(TOK, TOK), v(TOK, TOK),
            v(CHUNKS, TOK, LANES), b(TOK, 2 * NH), b(TOK, 2 * NH), b(TOK, 2 * NH),
            v(TOK, NH), v(TOK, NH), v(TOK, NH), v(TOK, NH), v(CHUNKS, PER, TOK),
            v(TOK, NH), v(TOK, NH), v(TOK, NH), v(8, NH), v(8, NH),
            b(TOK, 2 * NH), v(TOK, NH), v(TOK, NH), v(TOK, NH), v(TOK, NH), v(8, NH), buf(8), buf(8), buf(PAIRS, 8),
            b(NS, TOK), b(NS, TOK), b(NS, TOK), b(NS, 2 * NH), buf(8),
        ]
        + [buf(PAIRS, NS)] * 10
        + [
            buf(nx - 1, pa, NS), buf(ny - 1, pb, NS), buf(pa, NS), buf(pb, NS), buf(ny - 1, qa, NS),
            buf(nx - 1, qb, NS), buf(qa + qb, NS), buf(nz - 1, qa + qb, rows), buf(2 * (qa + qb), NS),
            buf(pa, NS), buf(pb, NS), buf(qa + qb, NS),
            buf(nz, 8), buf(ny, 8), buf(nx, 8), buf(nz, 8), buf(8), buf(8),
            buf(nx, 8), buf(ny, 8), buf(nz, 8), buf(2, 8), buf(8),
        ]
        + [sem(PAIRS)] * 4
        + [sem(nx + ny)] * 4
        + [sem(nz)] * 2
        + [sem(2 * nz)] * 2
        + [sem(2 * (nx + ny))] * 4
        + [sem(nx + ny), sem(2), sem(nx + ny), sem(2), sem(nz), sem(1)]
        + [sem(nz)] * 2 + [sem(ny)] * 2 + [sem(nx)] * 2 + [sem(nz)] * 2
        + [sem(nx)] * 2 + [sem(ny)] * 2 + [sem(nz)] * 2 + [sem(2)] * 2,
        compiler_params=pltpu.CompilerParams(collective_id=0, has_side_effects=True, vmem_limit_bytes=LIMIT),
        name="main",
    )(*args)


def body(
    mesh_shape,
    prompt_x, prompt_b, prompt_dt, prompt_states, resp_x, resp_b, resp_c, resp_dt, grad_out, lengths, advantages,
    dt_bias, a_log, skip,
):
    nz = mesh_shape["ctx"]
    px, pb, pdt = prompt_x[0], prompt_b[0], prompt_dt[0]
    ps = prompt_states.reshape(NH * HD, NS)
    rx, rb, rc, rdt, gy = resp_x[0, 0], resp_b[0, 0], resp_c[0, 0], resp_dt[0, 0], grad_out[0, 0]
    bias, alog = dt_bias[None], a_log[None]
    factor = advantages * float(nz * TOK) / lengths.astype(F32)
    pdx, pdb, pdd, rdx, rdb, rdc, rdd, small = main_call(
        mesh_shape, lengths, factor, rx, rb, rc, rdt.T, gy, px, pb, pdt.T, ps, bias, alog, skip[None],
    )
    return (
        pdx[None], pdb[None], pdd.T[None], rdx[None, None], rdb[None, None], rdc[None, None], rdd.T[None, None],
        small[0, :NH], small[1, :NH], small[2, :NH],
    )


def solution(mesh):
    wide = P("dp", ("ctx", "resp"), None)
    long = P("dp", "resp", "ctx", None)
    in_specs = (
        wide, wide, wide, P("dp", ("ctx", "resp"), None, None, None), long, long, long, long, long,
        P("dp", "resp"), P("dp", "resp"), P(), P(), P(),
    )
    out_specs = (wide, wide, wide, long, long, long, long, P(), P(), P())
    return jax.shard_map(
        functools.partial(body, dict(mesh.shape)), mesh=mesh, in_specs=in_specs, out_specs=out_specs, check_vma=False
    )
```

```python
import functools

import jax
import jax.numpy as jnp
from jax import lax
from jax.experimental import pallas as pl
from jax.experimental.pallas import tpu as pltpu
from jax.sharding import PartitionSpec as P

MESH = pl.DeviceIdType.MESH
F32 = jnp.float32
BF16 = jnp.bfloat16
TOK = 256
LANES = 256
PER = 4
NH = 64
HD = 64
NS = 128
CHUNKS = 16
PAIRS = 32
LIMIT = 56 * 1024 * 1024


def nn(a, b):
    return lax.dot_general(a, b, (((1,), (0,)), ((), ())), preferred_element_type=F32)


def nt(a, b):
    return lax.dot_general(a, b, (((1,), (1,)), ((), ())), preferred_element_type=F32)


def split2(v):
    hi = v.astype(BF16)
    return hi, (v - hi.astype(F32)).astype(BF16)


def split3(v):
    hi = v.astype(BF16)
    rest = v - hi.astype(F32)
    mid = rest.astype(BF16)
    return hi, mid, (rest - mid.astype(F32)).astype(BF16)


def exact_nn(tri, v):
    hi, mid, lo = split3(v)
    return nn(tri, hi) + (nn(tri, mid) + nn(tri, lo))


def iota(shape, dim):
    return lax.broadcasted_iota(jnp.int32, shape, dim)


def lower():
    return jnp.where(iota((TOK, TOK), 0) >= iota((TOK, TOK), 1), 1.0, 0.0).astype(BF16)


def upper():
    return jnp.where(iota((TOK, TOK), 0) <= iota((TOK, TOK), 1), 1.0, 0.0).astype(BF16)


def spreader(c, rows):
    head = iota((rows, LANES), 0) & (NH - 1)
    lane = iota((rows, LANES), 1) >> 6
    return jnp.where(head == lane + c * PER, 1.0, 0.0).astype(BF16)


def steps(dt, bias, alog):
    z = dt + bias
    d = jnp.maximum(z, 0.0) + jnp.log1p(jnp.exp(-jnp.abs(z)))
    rate = -jnp.exp(alog)
    a = exact_nn(lower(), rate * d)
    return z, d, rate, a


def cat2(v):
    hi, lo = split2(v)
    return jnp.concatenate([hi, lo], axis=1)


def by_head(v, spread):
    hi, lo = split2(v)
    return nt(hi, spread) + nt(lo, spread)


def fold8(v):
    total = v[0:8]
    for at in range(8, v.shape[0], 8):
        total = total + v[at : at + 8]
    return total


def cat3(v):
    return jnp.concatenate(split3(v), axis=1)


def column(v):
    return jnp.sum(v, axis=0, keepdims=True)


def triangle():
    return iota((TOK, TOK), 0) <= iota((TOK, TOK), 1)


def both(ref, c):
    return jnp.concatenate([ref[2 * c], ref[2 * c + 1]], axis=1)


def row_mask(length_ref):
    position = lax.axis_index("ctx") * TOK + iota((TOK, 1), 0)
    return jnp.where(position < length_ref[0, 0], 1.0, 0.0)


LAG = 3
LATE = 5
MARKS = (4, 5, 7, 9, 11, 13, 15)


def main_kernel(
    nz, nx, ny,
    len_ref, fac_ref,
    rx_ref, rb_ref, rc_ref, rdt_ref, gy_ref, px_ref, pb_ref, pdt_ref, ps_ref, bias_ref, alog_ref, skip_ref,
    pdx_ref, pdb_ref, pdd_ref, rdx_ref, rdb_ref, rdc_ref, rdd_ref, small_ref,
    a_ch, d_ch, a_t, gt, dgt, q1_ref, dcat, wcat, ecat, e_in, r_in, d_in, z_in, row, acc1, acc2, acc3, inner, outer,
    pwcat, pr, pd, pz, pacc, pinner, scan_ref, fol_ref, lanes_ref,
    bt, ct, pbt, pecat, tile_ref, fresh_ref, entry_ref, end_in,
    pre, suf, fsend, bsend, seedc, seed, end, ra, rb, sa, sb, ra2, rb2, own, rz, zfull, enda, endb, endown,
    tz, ty, tx, tp, mine_y, mine_x, sx, sy, sz, sd, terms,
    fs, fr, bs, br, s1, r1, s2, r2, s3, r3, s4, r4, s5, r5, s6, r6, e1s, e1r, e2s, e2r, e3s, e3r,
    tzs, tzr, tys, tyr, txs, txr, tps, tpr, xs_s, xs_r, ys_s, ys_r, zs_s, zs_r, ds_s, ds_r,
):
    dp, z, r = lax.axis_index("dp"), lax.axis_index("ctx"), lax.axis_index("resp")
    ndp = lax.axis_size("dp")
    x, y = r // ny, lax.rem(r, ny)
    half = PAIRS // 2
    pa, pb = half // nx, half // ny
    qa, qb = pa // ny, pb // nx
    rows = NS // nz
    dev = lambda zz, xx, yy: (dp, zz, xx * ny + yy)
    xs = [lax.rem(x + i, nx) for i in range(1, nx)]
    ys = [lax.rem(y + i, ny) for i in range(1, ny)]
    zs = [lax.rem(z + i, nz) for i in range(1, nz)]
    ds = [(lax.rem(dp + i, ndp), z, r) for i in range(1, ndp)]
    factor = fac_ref[0, 0]

    barrier = pltpu.get_barrier_semaphore()
    partners = [dev(z, t, y) for t in xs] + [dev(z, x, t) for t in ys] + [dev(t, x, y) for t in zs] + ds
    for partner in partners:
        pl.semaphore_signal(barrier, inc=1, device_id=partner, device_id_type=MESH)

    bias, alog = bias_ref[...], alog_ref[...]

    def prepare():
        zz, d, _, a = steps(rdt_ref[...].T, bias, alog)
        z_in[...] = zz
        d_in[...] = d
        at = a.T
        for k in range(CHUNKS):
            a_ch[k] = a[:, k * PER : k * PER + PER]
            d_ch[k] = d[:, k * PER : k * PER + PER]
            a_t[k] = at[k * PER : k * PER + PER]
        e = jnp.exp(a)
        rr = jnp.exp(a[TOK - 1 :, :] - a)
        e_in[...] = e
        r_in[...] = rr
        dcat[...] = cat2(d)
        wcat[...] = cat2(rr * d)
        ecat[...] = cat2(e)
        tile_ref[...] = jnp.ones_like(tile_ref)
        tile_ref[0:1, :NH] = e[TOK - 1 :]
        zz, d, _, a = steps(pdt_ref[...].T, bias, alog)
        pz[...] = zz
        pd[...] = d
        rr = jnp.exp(a[TOK - 1 :, :] - a)
        pr[...] = rr
        pwcat[...] = cat2(rr * d)
        tile_ref[1:2, :NH] = jnp.exp(a[TOK - 1 :, :])
        bt[...] = rb_ref[...].astype(F32).T.astype(BF16)
        ct[...] = rc_ref[...].astype(F32).T.astype(BF16)

    def prepare_rest():
        scores = nt(rb_ref[...], rc_ref[...])
        gt[...] = jnp.where(triangle(), scores, 0.0)
        dgt[...] = jnp.zeros_like(dgt)
        for acc in (acc1, acc2, acc3, inner, outer, pacc, pinner, rdb_ref, rdc_ref, pdb_ref):
            acc[...] = jnp.zeros_like(acc)
        for c in range(CHUNKS):
            put(lanes_ref, c, to_lanes(tile_ref[:, :NH], c))

        @pl.when(z == 0)
        def _():
            pre[...] = jnp.zeros_like(pre)

        @pl.when(z == nz - 1)
        def _():
            suf[...] = jnp.zeros_like(suf)

    def to_lanes(v, c):
        return nn(cat3(v), spreader(c, 3 * NH))

    def put(ref, c, value):
        ref[2 * c] = value[:, :128]
        ref[2 * c + 1] = value[:, 128:]

    def chunk_of(ref, c):
        return ref[:, pl.ds(pl.multiple_of(c * LANES, LANES), LANES)]

    def masked(c):
        return chunk_of(gy_ref, c).astype(F32) * row_mask(len_ref)

    def add_entry(c):
        hi, lo = split2(nn(ecat[...], spreader(c, 2 * NH)) * masked(c))
        put(entry_ref, c, nn(ct[...], hi) + nn(ct[...], lo))

    def add_fresh(c):
        hi, lo = split2(nn(wcat[...], spreader(c, 2 * NH)) * chunk_of(rx_ref, c).astype(F32))
        put(fresh_ref, c, nn(bt[...], hi) + nn(bt[...], lo))

    def saved_state(c):
        eye = jnp.where(iota((NS, NS), 0) == iota((NS, NS), 1), 1.0, 0.0).astype(BF16)
        return nt(eye, ps_ref[pl.ds(pl.multiple_of(c * LANES, LANES), LANES), :])

    def last_state():
        pbt[...] = pb_ref[...].astype(F32).T.astype(BF16)
        pecat[...] = cat2(jnp.broadcast_to(tile_ref[1:2, :NH], (NS, NH)))

    def add_last(c):
        spread = spreader(c, 2 * NH)
        hi, lo = split2(nn(pwcat[...], spread) * chunk_of(px_ref, c).astype(F32))
        put(end_in, c, nn(pecat[...], spread) * saved_state(c) + (nn(pbt[...], hi) + nn(pbt[...], lo)))

    prepare()
    pl.semaphore_wait(barrier, len(partners))

    def copy(src, dst, send, recv, to):
        return pltpu.make_async_remote_copy(
            src_ref=src, dst_ref=dst, send_sem=send, recv_sem=recv, device_id=to, device_id_type=MESH
        )

    def start(copies):
        for one in copies:
            one.start()

    def wait_send(copies):
        for one in copies:
            one.wait_send()

    def wait_recv(copies):
        for one in copies:
            one.wait_recv()

    def tiles_z():
        return [copy(tile_ref, tz.at[i], tzs.at[i], tzr.at[i], dev(t, x, y)) for i, t in enumerate(zs)]

    def tiles_y():
        return [copy(tile_ref, ty.at[i], tys.at[i], tyr.at[i], dev(z, x, t)) for i, t in enumerate(ys)]

    def tiles_x():
        return [copy(mine_y, tx.at[i], txs.at[i], txr.at[i], dev(z, t, y)) for i, t in enumerate(xs)]

    def tiles_p():
        return [copy(mine_x, tp.at[i], tps.at[i], tpr.at[i], dev(t, x, y)) for i, t in enumerate(zs)]

    def before(slots, at, size):
        total = jnp.ones((8, 128), F32)
        for i in range(size - 1):
            total = total * jnp.where(i + 1 <= at, slots[i], 1.0)
        return total

    def after(slots, at, size):
        total = jnp.ones((8, 128), F32)
        for i in range(size - 1):
            total = total * jnp.where(i + 1 > at, slots[i], 1.0)
        return total

    def phase1():
        return [
            copy(seedc.at[pl.ds(t * pa, pa)], ra.at[i], s1.at[i], r1.at[i], dev(z, t, y))
            for i, t in enumerate(xs)
        ] + [
            copy(seedc.at[pl.ds(half + t * pb, pb)], rb.at[i], s1.at[nx + i], r1.at[nx + i], dev(z, x, t))
            for i, t in enumerate(ys)
        ]

    def phase2():
        return [
            copy(sa.at[pl.ds(t * qa, qa)], ra2.at[i], s2.at[i], r2.at[i], dev(z, x, t))
            for i, t in enumerate(ys)
        ] + [
            copy(sb.at[pl.ds(t * qb, qb)], rb2.at[i], s2.at[ny + i], r2.at[ny + i], dev(z, t, y))
            for i, t in enumerate(xs)
        ]

    def phase3():
        return [
            copy(own.at[:, pl.ds(t * rows, rows)], rz.at[i], s3.at[i], r3.at[i], dev(t, x, y))
            for i, t in enumerate(zs)
        ]

    def phase4(k):
        mine = zfull.at[pl.ds(k * (qa + qb), qa + qb), pl.ds(z * rows, rows)]
        return [copy(mine, mine, s4.at[k * nz + i], r4.at[k * nz + i], dev(t, x, y)) for i, t in enumerate(zs)]

    la, lb = x * pa + y * qa, half + y * pb + x * qb

    def phase5(k):
        whole, found = (seed, end)[k], []
        for i, t in enumerate(ys):
            at, src = k * (nx + ny) + i, zfull.at[pl.ds(k * (qa + qb), qa)]
            found.append(copy(src, whole.at[pl.ds(la, qa)], s5.at[at], r5.at[at], dev(z, x, t)))
        for i, t in enumerate(xs):
            at, src = k * (nx + ny) + ny + i, zfull.at[pl.ds(k * (qa + qb) + qa, qb)]
            found.append(copy(src, whole.at[pl.ds(lb, qb)], s5.at[at], r5.at[at], dev(z, t, y)))
        return found

    def phase6(k):
        whole, found = (seed, end)[k], []
        for i, t in enumerate(xs):
            at, mine = k * (nx + ny) + i, whole.at[pl.ds(x * pa, pa)]
            found.append(copy(mine, mine, s6.at[at], r6.at[at], dev(z, t, y)))
        for i, t in enumerate(ys):
            at, mine = k * (nx + ny) + nx + i, whole.at[pl.ds(half + y * pb, pb)]
            found.append(copy(mine, mine, s6.at[at], r6.at[at], dev(z, x, t)))
        return found

    on_plane = z == nz - 1
    on_x, on_y = on_plane & (x == nx - 1), on_plane & (y == ny - 1)
    source = on_x & on_y

    def end1a(i, t):
        return copy(end_in.at[pl.ds(t * pa, pa)], enda, e1s.at[i], e1r.at[0], dev(z, t, y))

    def end1b(i, t):
        return copy(end_in.at[pl.ds(half + t * pb, pb)], endb, e1s.at[nx + i], e1r.at[1], dev(z, x, t))

    def end1():
        return [end1a(i, t) for i, t in enumerate(xs)] + [end1b(i, t) for i, t in enumerate(ys)]

    def end2a(i, t):
        return copy(enda.at[pl.ds(t * qa, qa)], endown.at[pl.ds(0, qa)], e2s.at[i], e2r.at[0], dev(z, x, t))

    def end2b(i, t):
        return copy(endb.at[pl.ds(t * qb, qb)], endown.at[pl.ds(qa, qb)], e2s.at[ny + i], e2r.at[1], dev(z, t, y))

    def end3(i, t):
        at = pl.ds(t * rows, rows)
        return copy(
            endown.at[:, at], zfull.at[pl.ds(qa + qb, qa + qb), at], e3s.at[i], e3r.at[0], dev(t, x, y)
        )

    def each(make, targets):
        return [make(i, t) for i, t in enumerate(targets)]

    def do1():
        wait_recv(tiles_z())
        scan = before(tz, z, nz)
        scan_ref[...] = scan
        for c in range(CHUNKS):
            wide = to_lanes(scan[:, :NH] * factor, c)
            seedc[2 * c] = entry_ref[2 * c] * wide[0:1, :128]
            seedc[2 * c + 1] = entry_ref[2 * c + 1] * wide[0:1, 128:]
        start(phase1())
        wait_recv(tiles_y())
        fol_ref[...] = after(ty, y, ny)
        total = tile_ref[...]
        for i in range(ny - 1):
            total = total * ty[i]
        mine_y[...] = total
        start(tiles_x())

        @pl.when(source)
        def _():
            last_state()

    def end_1():
        @pl.when(source)
        def _():
            start(end1())

    def do2():
        wait_recv(phase1())
        for q in range(pa):
            total = seedc[x * pa + q]
            for i in range(nx - 1):
                total = total + ra[i, q]
            sa[q] = total
        for q in range(pb):
            total = seedc[half + y * pb + q]
            for i in range(ny - 1):
                total = total + rb[i, q]
            sb[q] = total
        start(phase2())
        wait_recv(tiles_x())
        fol_ref[...] = fol_ref[...] * after(tx, x, nx)
        total = mine_y[...]
        for i in range(nx - 1):
            total = total * tx[i]
        mine_x[...] = total
        start(tiles_p())

    def end_2():
        @pl.when(source)
        def _():
            enda[...] = end_in[pl.ds(x * pa, pa)]
            endb[...] = end_in[pl.ds(half + y * pb, pb)]

        @pl.when(on_y)
        def _():
            @pl.when(x != nx - 1)
            def _():
                end1a(0, xs[0]).wait_recv()

            start(each(end2a, ys))
            for q in range(qa):
                endown[q] = enda[y * qa + q]

        @pl.when(on_x)
        def _():
            @pl.when(y != ny - 1)
            def _():
                end1b(0, ys[0]).wait_recv()

            start(each(end2b, xs))
            for q in range(qb):
                endown[qa + q] = endb[x * qb + q]

    def do3():
        wait_recv(phase2())
        wait_send(phase1())
        for q in range(qa):
            total = sa[y * qa + q]
            for i in range(ny - 1):
                total = total + ra2[i, q]
            own[q] = total
        for q in range(qb):
            total = sb[x * qb + q]
            for i in range(nx - 1):
                total = total + rb2[i, q]
            own[qa + q] = total
        start(phase3())

    def end_3():
        @pl.when(on_plane)
        def _():
            @pl.when(y != ny - 1)
            def _():
                end2a(0, ys[0]).wait_recv()

            @pl.when(x != nx - 1)
            def _():
                end2b(0, xs[0]).wait_recv()

            start(each(end3, zs))
            mine = pl.ds(z * rows, rows)
            for q in range(qa + qb):
                zfull[qa + qb + q, mine] = endown[q, mine]

    def do4():
        wait_recv(phase3())
        mine = pl.ds(z * rows, rows)
        for q in range(qa + qb):
            total = own[q, mine]
            for i in range(nz - 1):
                total = total + rz[i, q]
            zfull[q, mine] = total
        start(phase4(0))
        wait_recv(tiles_p())
        fol_ref[...] = fol_ref[...] * after(tp, z, nz)

    def end_4():
        @pl.when(jnp.logical_not(on_plane))
        def _():
            end3(0, zs[0]).wait_recv()

        start(phase4(1))

    def spread_5(k):
        whole = (seed, end)[k]
        wait_recv(phase4(k))
        start(phase5(k))
        for q in range(qa):
            whole[la + q] = zfull[k * (qa + qb) + q]
        for q in range(qb):
            whole[lb + q] = zfull[k * (qa + qb) + qa + q]

    def spread_6(k):
        wait_recv(phase5(k))
        start(phase6(k))

    def drain():
        for phase in (phase2, phase3, tiles_z, tiles_y, tiles_x, tiles_p):
            wait_send(phase())
        for phase in (phase4, phase5, phase6):
            wait_send(phase(0))
            wait_send(phase(1))

        @pl.when(source)
        def _():
            wait_send(end1())

        @pl.when(on_y)
        def _():
            wait_send(each(end2a, ys))

        @pl.when(on_x)
        def _():
            wait_send(each(end2b, xs))

        @pl.when(on_plane)
        def _():
            wait_send(each(end3, zs))

        def finish(q, carry):
            @pl.when(z < nz - 1)
            def _():
                forward(q).wait_send()

            @pl.when(z > 0)
            def _():
                backward(q).wait_send()

            return carry

        lax.fori_loop(0, PAIRS, finish, 0)

    def forward(q):
        return copy(fsend.at[q], pre.at[q], fs.at[q], fr.at[q], dev(lax.rem(z + 1, nz), x, y))

    def backward(q):
        return copy(bsend.at[q], suf.at[q], bs.at[q], br.at[q], dev(lax.rem(z + nz - 1, nz), x, y))

    def step(i):
        cf = i - LAG * z

        @pl.when((cf >= 0) & (cf < PAIRS))
        def _():
            @pl.when(z > 0)
            def _():
                forward(cf).wait_recv()

            @pl.when(z < nz - 1)
            def _():
                fsend[cf] = lanes_ref[cf, 0:1] * pre[cf] + fresh_ref[cf]
                forward(cf).start()

        cb = i - LAG * (nz - 1 - z)

        @pl.when((cb >= 0) & (cb < PAIRS))
        def _():
            @pl.when(z < nz - 1)
            def _():
                backward(cb).wait_recv()

            @pl.when(z > 0)
            def _():
                bsend[cb] = lanes_ref[cb, 0:1] * suf[cb] + entry_ref[cb]
                backward(cb).start()

    def alone(c):
        spread = spreader(c, NH)
        x_c = chunk_of(rx_ref, c)
        gf = masked(c)
        gy = gf.astype(BF16)
        xf = x_c.astype(F32)
        lane = iota((1, 128), 1) < HD
        q1 = []
        for pair in range(2):
            xp, gp = x_c[:, pair * 128 : pair * 128 + 128], gy[:, pair * 128 : pair * 128 + 128]
            total = [None] * 4
            for odd in range(2):
                j = 2 * pair + odd
                mine = jnp.logical_not(lane) if odd else lane
                xh = jnp.where(mine, xp, jnp.zeros_like(xp))
                gh = jnp.where(mine, gp, jnp.zeros_like(gp))
                col, dcol, arow = a_ch[c, :, j : j + 1], d_ch[c, :, j : j + 1], a_t[c, j : j + 1, :]
                found = [None, None]
                for b in range(4):
                    t0 = (b // 2) * 128
                    sl = slice(b * 64, b * 64 + 64)
                    g = gt[sl, t0:]
                    decay = jnp.exp(jnp.minimum(arow[:, t0:] - col[sl], 0.0))
                    hi, lo = split2(decay * g)
                    gpart = gh[t0:]
                    q = nn(hi, gpart) + nn(lo, gpart)
                    total[b] = q if total[b] is None else total[b] + q
                    k = decay * nt(xh[sl], gpart) * dcol[sl]
                    dgt[sl, t0:] += k
                    part = column(k * g)
                    at = b // 2
                    found[at] = part if found[at] is None else found[at] + part
                row[c, j : j + 1, :] = found[0]
                row[c, j : j + 1, 128:] += found[1]
            q1.append(jnp.concatenate(total, axis=0))
        q1 = jnp.concatenate(q1, axis=1)
        q1_ref[c] = q1
        acc1[...] += by_head(xf * q1, spread)
        outer[...] += by_head(fold8(xf * gf), spread)

    def with_grad(c):
        spread2 = spreader(c, 2 * NH)
        spread = spread2[:NH]
        xf = chunk_of(rx_ref, c).astype(F32)
        gf = masked(c)
        ghi, glo = split2(both(suf, c))
        rb_ = rb_ref[...]
        q2 = nn(rb_, ghi) + nn(rb_, glo)
        wide_w = nn(wcat[...], spread2)
        wide_skip = to_lanes(jnp.broadcast_to(skip_ref[...], (8, NH)), c)[0:1]
        found = factor * (nn(dcat[...], spread2) * q1_ref[c] + wide_w * q2 + wide_skip * gf)
        rdx_ref[:, pl.ds(pl.multiple_of(c * LANES, LANES), LANES)] = found.astype(BF16)
        acc2[...] += by_head(xf * q2, spread)
        whi, wlo = split2(wide_w * xf)
        rdb_ref[...] += nt(whi, ghi) + (nt(wlo, ghi) + nt(whi, glo))

    def with_state(c):
        spread2 = spreader(c, 2 * NH)
        spread = spread2[:NH]
        gf = masked(c)
        state = to_lanes(scan_ref[:, :NH], c)[0:1] * both(end, c) + both(pre, c)
        shi, slo = split2(state)
        rc_ = rc_ref[...]
        cs = nn(rc_, shi) + nn(rc_, slo)
        acc3[...] += by_head(gf * cs, spread)
        ehi, elo = split2(nn(ecat[...], spread2) * gf)
        rdc_ref[...] += nt(ehi, shi) + (nt(elo, shi) + nt(ehi, slo))
        inner[...] += by_head(fold8(state * both(suf, c)), spread)

    def prompt(c):
        spread = spreader(c, NH)
        pxf = chunk_of(px_ref, c).astype(F32)
        pgrad = to_lanes(fol_ref[:, :NH], c)[1:2] * both(seed, c)
        put(seedc, c, pgrad)
        ghi, glo = split2(pgrad)
        pb_ = pb_ref[...]
        q2 = nn(pb_, ghi) + nn(pb_, glo)
        q1_ref[c] = q2
        pacc[...] += by_head(pxf * q2, spread)
        pinner[...] += by_head(fold8(saved_state(c) * pgrad), spread)

    def prompt_rest(c):
        pxf = chunk_of(px_ref, c).astype(F32)
        ghi, glo = split2(both(seedc, c))
        wide_w = nn(pwcat[...], spreader(c, 2 * NH))
        pdx_ref[:, pl.ds(pl.multiple_of(c * LANES, LANES), LANES)] = (wide_w * q1_ref[c]).astype(BF16)
        whi, wlo = split2(wide_w * pxf)
        pdb_ref[...] += nt(whi, ghi) + (nt(wlo, ghi) + nt(whi, glo))

    rate = -jnp.exp(alog)

    def close(zz, d, dstep, da, last):
        cum = exact_nn(upper(), da) + last
        ddt = (dstep + rate * cum) / (1.0 + jnp.exp(-zz))
        return ddt, cum * (rate * d)

    def close_resp():
        d, rr, e = d_in[...], r_in[...], e_in[...]
        dstep = acc1[...] + rr * acc2[...]
        erow = jnp.concatenate([row[k] for k in range(CHUNKS)], axis=0).T
        da = erow + e * acc3[...] - d * dstep
        last = e[TOK - 1 :] * column(inner[...]) + column(rr * d * acc2[...])
        ddt, dalog = close(z_in[...], d, dstep, da, last)
        ddt = factor * ddt
        rdd_ref[...] = ddt.T
        terms[...] = jnp.zeros_like(terms)
        terms[0:1, :NH] = column(ddt)
        terms[1:2, :NH] = factor * column(dalog)
        terms[2:3, :NH] = factor * column(outer[...])

    def close_prompt():
        d, rr = pd[...], pr[...]
        dstep = rr * pacc[...]
        weighted = d * dstep
        last = jnp.exp(column(rate * d)) * column(pinner[...]) + column(weighted)
        ddt, dalog = close(pz[...], d, dstep, -weighted, last)
        pdd_ref[...] = ddt.T
        terms[0:1, :NH] += column(ddt)
        terms[1:2, :NH] += column(dalog)

    def scores():
        keep = jnp.where(triangle(), dgt[...], 0.0)
        hi, lo = split2(keep)
        rdb_ref[...] = factor * (rdb_ref[...] + (nn(hi, rc_ref[...]) + nn(lo, rc_ref[...])))
        hi, lo = split2(keep.T)
        rdc_ref[...] = factor * (rdc_ref[...] + (nn(hi, rb_ref[...]) + nn(lo, rb_ref[...])))

    def terms_of(slots, at, send, recv, targets):
        mine = slots.at[at]
        return [copy(mine, mine, send.at[i], recv.at[i], to) for i, to in enumerate(targets)]

    def gather(slots, at, size, send, recv, targets, beside):
        slots[at] = terms[...]
        copies = terms_of(slots, at, send, recv, targets)
        start(copies)
        beside()
        wait_recv(copies)
        total = slots[0]
        for i in range(1, size):
            total = total + slots[i]
        terms[...] = total
        return copies

    start(tiles_z())
    start(tiles_y())

    def looped(work, lo, hi, unroll=2):
        def one(c, carry):
            work(c)
            return carry

        lax.fori_loop(lo, hi, one, 0, unroll=unroll)

    looped(add_entry, 0, CHUNKS)
    do1()
    prepare_rest()
    first_full = -(-LAG * (nz - 1) // 2)
    turns = first_full + CHUNKS

    def turn(j, carry):
        @pl.when(j < CHUNKS)
        def _():
            add_fresh(j)

        step(2 * j)

        @pl.when(source & (j < 4))
        def _():
            for k in range(4):
                add_last(4 * j + k)

        @pl.when(j < CHUNKS)
        def _():
            alone(j)

        step(2 * j + 1)

        @pl.when(j >= first_full)
        def _():
            with_grad(j - first_full)

        return carry

    def late_turn(j, carry):
        turn(j, carry)
        k = j - (turns - LATE)

        for i in range(2):
            with_state(2 * k + i)
        for i in range(3):
            prompt(3 * k + i)
        return carry

    done = 0
    acts = (
        end_1, do2, lambda: (do3(), end_2()), lambda: (do4(), end_3()), lambda: (spread_5(0), end_4()),
        lambda: (spread_6(0), spread_5(1)), lambda: spread_6(1),
    )
    for mark, act in zip(MARKS, acts):
        mark = min(mark, turns - LATE)
        lax.fori_loop(done, mark, turn, 0)
        act()
        done = mark
    lax.fori_loop(done, turns - LATE, turn, 0)
    wait_recv(phase6(0))
    wait_recv(phase6(1))
    lax.fori_loop(turns - LATE, turns, late_turn, 0)
    looped(with_state, 2 * LATE, CHUNKS)
    looped(prompt, 3 * LATE, CHUNKS)
    close_resp()
    close_prompt()
    part = CHUNKS // 4
    pending = gather(sx, x, nx, xs_s, xs_r, [dev(z, t, y) for t in xs], lambda: looped(prompt_rest, 0, part))
    pending += gather(
        sy, y, ny, ys_s, ys_r, [dev(z, x, t) for t in ys], lambda: looped(prompt_rest, part, 2 * part)
    )
    pending += gather(
        sz, z, nz, zs_s, zs_r, [dev(t, x, y) for t in zs], lambda: looped(prompt_rest, 2 * part, CHUNKS)
    )
    pending += gather(sd, dp, ndp, ds_s, ds_r, ds, scores)
    small_ref[...] = terms[...]
    wait_send(pending)
    drain()


def factors(count):
    first = 1
    while first * first < count:
        first *= 2
    return first, count // first


def main_call(mesh_shape, *args):
    nz = mesh_shape["ctx"]
    nx, ny = factors(mesh_shape["resp"])
    half = PAIRS // 2
    pa, pb = half // nx, half // ny
    qa, qb = pa // ny, pb // nx
    rows = NS // nz
    vmem = pl.BlockSpec(memory_space=pltpu.VMEM)
    smem = pl.BlockSpec(memory_space=pltpu.SMEM)
    v = lambda *shape: pltpu.VMEM(shape, F32)
    b = lambda *shape: pltpu.VMEM(shape, BF16)
    buf = lambda *lead: pltpu.VMEM(lead + (128,), F32)
    sem = lambda n: pltpu.SemaphoreType.DMA((n,))
    return pl.pallas_call(
        functools.partial(main_kernel, nz, nx, ny),
        out_shape=(
            b(TOK, NH * HD), v(TOK, NS), v(NH, TOK), b(TOK, NH * HD), v(TOK, NS), v(TOK, NS), v(NH, TOK), v(8, 128),
        ),
        in_specs=[smem] * 2 + [vmem] * 12,
        out_specs=(vmem,) * 8,
        scratch_shapes=[
            v(CHUNKS, TOK, PER), v(CHUNKS, TOK, PER), v(CHUNKS, PER, TOK), v(TOK, TOK), v(TOK, TOK),
            v(CHUNKS, TOK, LANES), b(TOK, 2 * NH), b(TOK, 2 * NH), b(TOK, 2 * NH),
            v(TOK, NH), v(TOK, NH), v(TOK, NH), v(TOK, NH), v(CHUNKS, PER, TOK),
            v(TOK, NH), v(TOK, NH), v(TOK, NH), v(8, NH), v(8, NH),
            b(TOK, 2 * NH), v(TOK, NH), v(TOK, NH), v(TOK, NH), v(TOK, NH), v(8, NH), buf(8), buf(8), buf(PAIRS, 8),
            b(NS, TOK), b(NS, TOK), b(NS, TOK), b(NS, 2 * NH), buf(8),
        ]
        + [buf(PAIRS, NS)] * 10
        + [
            buf(nx - 1, pa, NS), buf(ny - 1, pb, NS), buf(pa, NS), buf(pb, NS), buf(ny - 1, qa, NS),
            buf(nx - 1, qb, NS), buf(qa + qb, NS), buf(nz - 1, qa + qb, rows), buf(2 * (qa + qb), NS),
            buf(pa, NS), buf(pb, NS), buf(qa + qb, NS),
            buf(nz, 8), buf(ny, 8), buf(nx, 8), buf(nz, 8), buf(8), buf(8),
            buf(nx, 8), buf(ny, 8), buf(nz, 8), buf(2, 8), buf(8),
        ]
        + [sem(PAIRS)] * 4
        + [sem(nx + ny)] * 4
        + [sem(nz)] * 2
        + [sem(2 * nz)] * 2
        + [sem(2 * (nx + ny))] * 4
        + [sem(nx + ny), sem(2), sem(nx + ny), sem(2), sem(nz), sem(1)]
        + [sem(nz)] * 2 + [sem(ny)] * 2 + [sem(nx)] * 2 + [sem(nz)] * 2
        + [sem(nx)] * 2 + [sem(ny)] * 2 + [sem(nz)] * 2 + [sem(2)] * 2,
        compiler_params=pltpu.CompilerParams(collective_id=0, has_side_effects=True, vmem_limit_bytes=LIMIT),
        name="main",
    )(*args)


def body(
    mesh_shape,
    prompt_x, prompt_b, prompt_dt, prompt_states, resp_x, resp_b, resp_c, resp_dt, grad_out, lengths, advantages,
    dt_bias, a_log, skip,
):
    nz = mesh_shape["ctx"]
    px, pb, pdt = prompt_x[0], prompt_b[0], prompt_dt[0]
    ps = prompt_states.reshape(NH * HD, NS)
    rx, rb, rc, rdt, gy = resp_x[0, 0], resp_b[0, 0], resp_c[0, 0], resp_dt[0, 0], grad_out[0, 0]
    bias, alog = dt_bias[None], a_log[None]
    factor = advantages * float(nz * TOK) / lengths.astype(F32)
    pdx, pdb, pdd, rdx, rdb, rdc, rdd, small = main_call(
        mesh_shape, lengths, factor, rx, rb, rc, rdt.T, gy, px, pb, pdt.T, ps, bias, alog, skip[None],
    )
    return (
        pdx[None], pdb[None], pdd.T[None], rdx[None, None], rdb[None, None], rdc[None, None], rdd.T[None, None],
        small[0, :NH], small[1, :NH], small[2, :NH],
    )


def solution(mesh):
    wide = P("dp", ("ctx", "resp"), None)
    long = P("dp", "resp", "ctx", None)
    in_specs = (
        wide, wide, wide, P("dp", ("ctx", "resp"), None, None, None), long, long, long, long, long,
        P("dp", "resp"), P("dp", "resp"), P(), P(), P(),
    )
    out_specs = (wide, wide, wide, long, long, long, long, P(), P(), P())
    return jax.shard_map(
        functools.partial(body, dict(mesh.shape)), mesh=mesh, in_specs=in_specs, out_specs=out_specs, check_vma=False
    )
```
